512 devices in a mesh: blk: 16 (over z_hi, y, core), fsdp: 32 (over z_lo, x).
Axes of the slice: x: 4, y: 4, z: 16 (z_hi: 2, z_lo: 8; z = z_hi * 8 + z_lo), core: 2. Of those that a mesh axis runs over, the one named last changes fastest.
Arguments:
- tokens: bfloat16 [16, 4096, 8192], P('blk', 'fsdp'), may hold values from -6 to 6
- norm_gain: float32 [8192], replicated, may hold values from 0.1 to 1.9
- adapt_in: float32 [16, 8192, 64], P('blk', 'fsdp'), may hold values from -6 to 6
- adapt_out: float32 [16, 8192, 64], P('blk', 'fsdp'), may hold values from -6 to 6
- upstream: bfloat16 [16, 4096, 8192], P('blk', 'fsdp'), may hold values from -6 to 6
Outputs:
- mixed_in: float32 [16, 8192, 64], P('blk', 'fsdp')
- mixed_out: float32 [16, 8192, 64], P('blk', 'fsdp')
The draws below stay inside these ranges and needn't reach their ends.
All inputs are finite; a program needn't handle non-finite values.
Results may differ from the reference program's by a relative error of at most 0.0029.
Values may be sent and summed in bfloat16 or wider, within the bound.
No kernel may reach another device: no remote copies, remote signals or barrier semaphores. Data moves between devices by JAX's collectives and lax.ppermute only.
A program may use at most 64 MiB of HBM per device.

```python
import jax
import jax.numpy as jnp
from jax import lax

D = 8192
R = 64
TOKENS = 4096
GROUPS = 16


def block_levels(key, dims, pieces, low, high):
    factor_of, own = 1.0, jax.random.fold_in(key, 6)
    for position, parts in pieces:
        steps = jnp.exp(jax.random.uniform(jax.random.fold_in(own, position), (parts,), jnp.float32, low / len(pieces), high / len(pieces)))
        factor_of = factor_of * jnp.repeat(steps, dims[position] // parts).reshape([-1 if axis == position else 1 for axis in range(len(dims))])
    return factor_of


def normal_values(key, extent, deviation, most, cuts=(), held_as=jnp.bfloat16):
    factor_of = block_levels(key, extent, cuts, -0.22, 0.18) if cuts else 1.0
    entries = jax.random.normal(key, extent, jnp.float32) * deviation * factor_of
    return jnp.minimum(jnp.maximum(entries, -most), most).astype(held_as)


def setup_inputs(seed: int = 0) -> dict:
    key_list = jax.random.split(jax.random.key(seed), 6)
    return {
        "tokens": normal_values(key_list[0], (GROUPS, TOKENS, D), 1.0, 6.0, ((0, 16), (1, 32))),
        "norm_gain": jnp.clip(1.0 + 0.18 * jax.random.normal(key_list[1], (D,), jnp.float32), 0.1, 1.9),
        "adapt_in": normal_values(key_list[2], (GROUPS, D, R), 1.0, 6.0, ((0, 16), (1, 32)), jnp.float32),
        "adapt_out": normal_values(key_list[3], (GROUPS, D, R), 1.0, 6.0, ((0, 16), (1, 32)), jnp.float32),
        "upstream": normal_values(key_list[4], (GROUPS, TOKENS, D), 1.0, 6.0, ((0, 16), (1, 32))),
    }


learning_rate = 4.0
epsilon = 1e-05

def group_step(carry_args, norm_gain):
    tokens, adapt_in, adapt_out, upstream = carry_args
    inv_width = D ** (-0.5)
    inv_rank = R ** (-0.5)
    wide = tokens.astype(jnp.float32)
    normed = (wide * lax.rsqrt(lax.optimization_barrier(jnp.mean(wide * wide, axis=-1, keepdims=True)) + epsilon) * norm_gain).astype(jnp.bfloat16)
    low_in = adapt_in.astype(jnp.bfloat16)
    low_out = adapt_out.astype(jnp.bfloat16)
    factor = (jnp.dot(normed, low_in, preferred_element_type=jnp.float32) * inv_width).astype(jnp.bfloat16)
    pulled = (jnp.dot(upstream, low_out, preferred_element_type=jnp.float32) * inv_rank).astype(jnp.bfloat16)
    contract = (((0,), (0,)), ((), ()))
    grad_in = lax.dot_general(normed, pulled, contract, preferred_element_type=jnp.float32) * inv_width
    grad_out = lax.dot_general(upstream, factor, contract, preferred_element_type=jnp.float32) * inv_rank
    step_size = learning_rate / TOKENS ** 0.5
    return (adapt_in - step_size * grad_in, adapt_out - step_size * grad_out)

def reference(tokens, norm_gain, adapt_in, adapt_out, upstream):
    stepped_in, stepped_out = lax.map(lambda group: group_step(group, norm_gain), (tokens, adapt_in, adapt_out, upstream))
    mixed_in = (jnp.roll(stepped_in, 1, axis=0) + stepped_in + jnp.roll(stepped_in, -1, axis=0)) / 3.0
    mixed_out = (jnp.roll(stepped_out, 1, axis=0) + stepped_out + jnp.roll(stepped_out, -1, axis=0)) / 3.0
    return (mixed_in, mixed_out)
```

```python
import jax
import jax.numpy as jnp
from jax import lax
from jax.experimental import pallas as pl
from jax.experimental.pallas import tpu as pltpu
from jax.sharding import Mesh
from jax.sharding import PartitionSpec as P

D = 8192
R = 64
TOKENS = 4096
GROUPS = 16
NX = 4
NZ = 8
TOK = TOKENS // (NX * NZ)
OWN = D // (NX * NZ)
FEAT = D // NX

learning_rate = 4.0
epsilon = 1e-05

inv_width = D ** (-0.5)
inv_rank = R ** (-0.5)
step_size = learning_rate / TOKENS**0.5

LAST = (((1,), (1,)), ((), ()))
VMEM_LIMIT = 40 * 1024 * 1024


def prep_kernel(tok_ref, gain_ref, up_ref, out_ref):
    wide = tok_ref[...].astype(jnp.float32)
    scale = lax.rsqrt(jnp.mean(wide * wide, axis=-1, keepdims=True) + epsilon)
    for x in range(NX):
        for z in range(NZ):
            src = slice((z * NX + x) * OWN, (z * NX + x + 1) * OWN)
            dst = slice(z * OWN, (z + 1) * OWN)
            part = tok_ref[:, src].astype(jnp.float32) * scale * gain_ref[:, src]
            out_ref[x, 0, :, dst] = part.astype(jnp.bfloat16)
            out_ref[x, 1, :, dst] = up_ref[:, src]


def prep(tokens, gain, upstream):
    rows = 32
    return pl.pallas_call(
        prep_kernel,
        grid=(TOK // rows,),
        in_specs=[
            pl.BlockSpec((rows, D), lambda i: (i, 0)),
            pl.BlockSpec((1, D), lambda i: (0, 0)),
            pl.BlockSpec((rows, D), lambda i: (i, 0)),
        ],
        out_specs=pl.BlockSpec((NX, 2, rows, FEAT), lambda i: (0, 0, i, 0)),
        out_shape=jax.ShapeDtypeStruct((NX, 2, TOK, FEAT), jnp.bfloat16),
        compiler_params=pltpu.CompilerParams(vmem_limit_bytes=VMEM_LIMIT),
        cost_estimate=pl.CostEstimate(
            flops=6 * TOK * D, bytes_accessed=8 * TOK * D, transcendentals=TOK
        ),
    )(tokens, gain, upstream)


def project_kernel(feat_ref, low_ref, out_ref):
    low = jnp.concatenate([low_ref[z] for z in range(NZ)], axis=1).astype(jnp.bfloat16)
    fac = lax.dot_general(low[:R], feat_ref[0, 0], LAST, preferred_element_type=jnp.float32)
    pul = lax.dot_general(low[R:], feat_ref[0, 1], LAST, preferred_element_type=jnp.float32)
    for x in range(NX):
        out_ref[x, 0, :R, :] = fac
        out_ref[x, 0, R:, :] = pul


def project(feat, low):
    return pl.pallas_call(
        project_kernel,
        grid=(NX,),
        in_specs=[
            pl.BlockSpec((1, 2, TOK, FEAT), lambda i: (i, 0, 0, 0)),
            pl.BlockSpec((NZ, 2 * R, OWN), lambda i: (0, 0, 0)),
        ],
        out_specs=pl.BlockSpec((NX, 1, 2 * R, TOK), lambda i: (0, i, 0, 0)),
        out_shape=jax.ShapeDtypeStruct((NX, NX, 2 * R, TOK), jnp.float32),
        compiler_params=pltpu.CompilerParams(vmem_limit_bytes=VMEM_LIMIT),
        cost_estimate=pl.CostEstimate(
            flops=4 * NX * TOK * FEAT * R, bytes_accessed=6 * 1024 * 1024, transcendentals=0
        ),
    )(feat, low)


def grads_kernel(part_ref, feat_ref, out_ref):
    total = part_ref[0]
    for x in range(1, NX):
        total = total + part_ref[x]
    fac = jnp.concatenate([total[s, :R] for s in range(NX)], axis=1) * inv_width
    pul = jnp.concatenate([total[s, R:] for s in range(NX)], axis=1) * inv_rank
    normed = feat_ref[:, 0].reshape(NX * TOK, OWN)
    cotangent = feat_ref[:, 1].reshape(NX * TOK, OWN)
    g_in = jnp.dot(pul.astype(jnp.bfloat16), normed, preferred_element_type=jnp.float32)
    g_out = jnp.dot(fac.astype(jnp.bfloat16), cotangent, preferred_element_type=jnp.float32)
    out_ref[0, :R, :] = (g_in * inv_width).astype(jnp.bfloat16)
    out_ref[0, R:, :] = (g_out * inv_rank).astype(jnp.bfloat16)


def grads(part, feat):
    return pl.pallas_call(
        grads_kernel,
        grid=(NZ,),
        in_specs=[
            pl.BlockSpec((NX, NX, 2 * R, TOK), lambda i: (0, 0, 0, 0)),
            pl.BlockSpec((NX, 2, TOK, OWN), lambda i: (0, 0, 0, i)),
        ],
        out_specs=pl.BlockSpec((1, 2 * R, OWN), lambda i: (i, 0, 0)),
        out_shape=jax.ShapeDtypeStruct((NZ, 2 * R, OWN), jnp.bfloat16),
        compiler_params=pltpu.CompilerParams(vmem_limit_bytes=VMEM_LIMIT),
        cost_estimate=pl.CostEstimate(
            flops=4 * NX * TOK * FEAT * R, bytes_accessed=6 * 1024 * 1024, transcendentals=0
        ),
    )(part, feat)


def shifted(array, by):
    return lax.ppermute(array, "blk", [(i, (i + by) % GROUPS) for i in range(GROUPS)])


def local(tokens, norm_gain, adapt_in, adapt_out, upstream):
    master = jnp.concatenate([adapt_in[0].T, adapt_out[0].T], axis=0)
    low = lax.all_gather(master[None], "z", axis=0, tiled=True)
    base = shifted(master, 1) + master + shifted(master, -1)

    feat = prep(tokens[0], norm_gain[None], upstream[0])
    feat = lax.all_to_all(feat, "x", 0, 0, tiled=True)
    part = project(feat, low)
    part = lax.all_to_all(part, "x", 0, 0, tiled=True)
    pieces = grads(part, feat)
    pieces = lax.all_to_all(pieces, "z", 0, 0, tiled=True)
    grad = jnp.sum(pieces.astype(jnp.float32), axis=0)
    sent = grad.astype(jnp.bfloat16)
    lower, upper = shifted(sent, 1), shifted(sent, -1)
    around = lower.astype(jnp.float32) + grad + upper.astype(jnp.float32)
    mixed = (base - step_size * around) / 3.0
    return (mixed[:R].T[None], mixed[R:].T[None])


def solution(mesh):
    mesh = Mesh(mesh.devices.reshape(GROUPS, NZ, NX), ("blk", "z", "x"))
    split = P("blk", ("z", "x"), None)
    in_specs = (split, P(), split, split, split)
    return jax.shard_map(
        local, mesh=mesh, in_specs=in_specs, out_specs=(split, split), check_vma=False
    )
```

```python
import functools

import jax
import jax.numpy as jnp
from jax import lax
from jax.experimental import pallas as pl
from jax.experimental.pallas import tpu as pltpu
from jax.sharding import Mesh
from jax.sharding import PartitionSpec as P

D = 8192
R = 64
TOKENS = 4096
GROUPS = 16
NX = 4
NZ = 8
TOK = TOKENS // (NX * NZ)
OWN = D // (NX * NZ)
QUAD = NZ // 2
FEAT = D // NX

learning_rate = 4.0
epsilon = 1e-05

inv_width = D ** (-0.5)
inv_rank = R ** (-0.5)
step_size = learning_rate / TOKENS**0.5

LAST = (((1,), (1,)), ((), ()))
VMEM_LIMIT = 40 * 1024 * 1024
DIRECT_LIMIT = 60 * 1024 * 1024


def norm_kernel(tok_ref, gain_ref, out_ref):
    wide = tok_ref[...].astype(jnp.float32)
    scale = lax.rsqrt(jnp.mean(wide * wide, axis=-1, keepdims=True) + epsilon)
    for x in range(NX):
        for z in range(NZ):
            src = slice((z * NX + x) * OWN, (z * NX + x + 1) * OWN)
            part = tok_ref[:, src].astype(jnp.float32) * scale * gain_ref[:, src]
            out_ref[x, :, z * OWN : (z + 1) * OWN] = part.astype(jnp.bfloat16)


def split_kernel(up_ref, out_ref):
    for x in range(NX):
        for z in range(NZ):
            src = slice((z * NX + x) * OWN, (z * NX + x + 1) * OWN)
            out_ref[x, :, z * OWN : (z + 1) * OWN] = up_ref[:, src]


def prep(kernel, array, *gain):
    rows = 32
    return pl.pallas_call(
        kernel,
        grid=(TOK // rows,),
        in_specs=[pl.BlockSpec((rows, D), lambda i: (i, 0))]
        + [pl.BlockSpec((1, D), lambda i: (0, 0)) for _ in gain],
        out_specs=pl.BlockSpec((NX, rows, FEAT), lambda i: (0, i, 0)),
        out_shape=jax.ShapeDtypeStruct((NX, TOK, FEAT), jnp.bfloat16),
        compiler_params=pltpu.CompilerParams(vmem_limit_bytes=DIRECT_LIMIT),
        cost_estimate=pl.CostEstimate(
            flops=4 * TOK * D, bytes_accessed=4 * TOK * D, transcendentals=0
        ),
    )(array, *gain)


def project_kernel(row, feat_ref, *refs):
    low_refs, out_ref, low_ref = refs[:QUAD], refs[QUAD], refs[QUAD + 1]
    me = lax.axis_index("z")

    @pl.when(pl.program_id(0) == 0)
    def _():
        for near in range(QUAD):
            for far in range(2):
                at = pl.multiple_of((me ^ (near + QUAD * far)) * OWN, OWN)
                low_ref[:, pl.ds(at, OWN)] = low_refs[near][far, row : row + R]

    for s in range(2):
        part = lax.dot_general(low_ref[...], feat_ref[s], LAST, preferred_element_type=jnp.float32)
        for x in range(out_ref.shape[0]):
            out_ref[x, s] = part


def project(feat, lows, row, copies):
    return pl.pallas_call(
        functools.partial(project_kernel, row),
        grid=(NX // 2,),
        in_specs=[pl.BlockSpec((2, TOK, FEAT), lambda i: (i, 0, 0))]
        + [pl.BlockSpec((2, 2 * R, OWN), lambda i: (0, 0, 0)) for _ in lows],
        out_specs=pl.BlockSpec((copies, 2, R, TOK), lambda i: (0, i, 0, 0)),
        out_shape=jax.ShapeDtypeStruct((copies, NX, R, TOK), jnp.float32),
        scratch_shapes=[pltpu.VMEM((R, FEAT), jnp.bfloat16)],
        compiler_params=pltpu.CompilerParams(vmem_limit_bytes=VMEM_LIMIT),
        cost_estimate=pl.CostEstimate(
            flops=2 * NX * TOK * FEAT * R, bytes_accessed=3 * 1024 * 1024, transcendentals=0
        ),
    )(feat, *lows)


def grads_kernel(relative, scale_part, scale_grad, feat_ref, *refs):
    part_refs, out_ref, low_ref = refs[:-2], refs[-2], refs[-1]
    step = pl.program_id(0)

    @pl.when(step == 0)
    def _():
        for s in range(NX):
            terms = [ref[x, s] for ref in part_refs for x in range(ref.shape[0])]
            total = sum(terms[1:], terms[0])
            low_ref[:, s * TOK : (s + 1) * TOK] = (total * scale_part).astype(jnp.bfloat16)

    grad = jnp.dot(
        low_ref[...],
        feat_ref[...].reshape(NX * TOK, 2 * OWN),
        preferred_element_type=jnp.float32,
    )
    grad = (grad * scale_grad).astype(jnp.bfloat16)
    me = lax.axis_index("z") if relative else 0
    for half in range(2):
        out_ref[me ^ (2 * step + half)] = grad[:, half * OWN : (half + 1) * OWN]


def grads(parts, feat, scale_part, scale_grad, relative):
    return pl.pallas_call(
        functools.partial(grads_kernel, relative, scale_part, scale_grad),
        grid=(NZ // 2,),
        in_specs=[pl.BlockSpec((NX, TOK, 2 * OWN), lambda i: (0, 0, i))]
        + [pl.BlockSpec(part.shape, lambda i: (0, 0, 0, 0)) for part in parts],
        out_specs=pl.BlockSpec((NZ, R, OWN), lambda i: (0, 0, 0)),
        out_shape=jax.ShapeDtypeStruct((NZ, R, OWN), jnp.bfloat16),
        scratch_shapes=[pltpu.VMEM((R, NX * TOK), jnp.bfloat16)],
        compiler_params=pltpu.CompilerParams(vmem_limit_bytes=VMEM_LIMIT),
        cost_estimate=pl.CostEstimate(
            flops=2 * NX * TOK * FEAT * R, bytes_accessed=3 * 1024 * 1024, transcendentals=0
        ),
    )(feat, *parts)


def shifted(array, axis, by):
    count = lax.axis_size(axis)
    return lax.ppermute(array, axis, [(i, (i + by) % count) for i in range(count)])


def swapped(array, by):
    return lax.ppermute(array, "z", [(i, i ^ by) for i in range(NZ)])


def exchange(array, axis):
    return lax.all_to_all(array, axis, 0, 0, tiled=True)


def mix(base, grad):
    sent = grad.astype(jnp.bfloat16)
    lower, upper = shifted(sent, "blk", 1), shifted(sent, "blk", -1)
    around = lower.astype(jnp.float32) + grad + upper.astype(jnp.float32)
    return ((base - step_size * around) / 3.0).T[None]


def local(tokens, norm_gain, adapt_in, adapt_out, upstream):
    wide = jnp.float32
    cotangent = prep(split_kernel, upstream[0])
    cotangent, adapt_in, adapt_out = lax.optimization_barrier((cotangent, adapt_in, adapt_out))
    cotangent = exchange(cotangent, "x")

    master = jnp.concatenate([adapt_in[0].T, adapt_out[0].T], axis=0)
    own = master.astype(jnp.bfloat16)
    pair = jnp.stack([own, swapped(own, QUAD)])
    lows = [pair] + [swapped(pair, k) for k in range(1, QUAD)]

    normed = prep(norm_kernel, tokens[0], norm_gain[None])
    cotangent, normed, lows = lax.optimization_barrier((cotangent, normed, lows))
    normed = exchange(normed, "x")
    base = shifted(master, "blk", 1) + master + shifted(master, "blk", -1)

    mine = project(cotangent, lows, R, 1)
    pulled = [mine, shifted(mine, "x", 1), shifted(mine, "x", -1), shifted(mine, "x", 2)]
    normed, base, pulled = lax.optimization_barrier((normed, base, pulled))

    factor = exchange(project(normed, lows, 0, NX), "x")
    near = grads(pulled, normed, inv_rank, inv_width, True)
    near = near.reshape(2, QUAD, R, OWN)
    quad = near[:, 0].astype(wide)
    for k in range(1, QUAD):
        quad = quad + swapped(near[:, k], k).astype(wide)
    grad_in = quad[0] + swapped(quad[1], QUAD)

    pieces = exchange(grads([factor], cotangent, inv_width, inv_rank, False), "z")
    grad_out = jnp.sum(pieces.astype(wide), axis=0)
    return (mix(base[:R], grad_in), mix(base[R:], grad_out))


def solution(mesh):
    mesh = Mesh(mesh.devices.reshape(GROUPS, NZ, NX), ("blk", "z", "x"))
    split = P("blk", ("z", "x"), None)
    in_specs = (split, P(), split, split, split)
    return jax.shard_map(
        local, mesh=mesh, in_specs=in_specs, out_specs=(split, split), check_vma=False
    )
```

```python
import jax
import jax.numpy as jnp
from jax import lax
from jax.experimental import pallas as pl
from jax.experimental.pallas import tpu as pltpu
from jax.sharding import Mesh
from jax.sharding import PartitionSpec as P

D = 8192
R = 64
TOKENS = 4096
GROUPS = 16
NX = 4
NZ = 8
TOK = TOKENS // (NX * NZ)
OWN = D // (NX * NZ)
QUAD = NZ // 2
FEAT = D // NX

learning_rate = 4.0
epsilon = 1e-05

inv_width = D ** (-0.5)
inv_rank = R ** (-0.5)
step_size = learning_rate / TOKENS**0.5

ROWS = 32
CHUNKS = TOK // ROWS

LAST = (((1,), (1,)), ((), ()))
VMEM_LIMIT = 40 * 1024 * 1024
DIRECT_LIMIT = 60 * 1024 * 1024


def prep_kernel(tok_ref, gain_ref, up_ref, out_ref, raw_ref, done_ref, in_sem, out_sem, up_sem):
    loads = []
    for c in range(CHUNKS):
        rows = pl.ds(c * ROWS, ROWS)
        loads.append(pltpu.make_async_copy(tok_ref.at[rows], raw_ref.at[c], in_sem.at[c]))
        loads[-1].start()
    moves = []
    for b in range(NX * NZ):
        z, x = divmod(b, NX)
        src = up_ref.at[:, pl.ds(b * OWN, OWN)]
        dst = out_ref.at[x, 1, :, pl.ds(z * OWN, OWN)]
        moves.append(pltpu.make_async_copy(src, dst, up_sem.at[b]))
        moves[-1].start()
    stores = []
    for c in range(CHUNKS):
        loads[c].wait()
        wide = raw_ref[c].astype(jnp.float32)
        scale = lax.rsqrt(jnp.mean(wide * wide, axis=-1, keepdims=True) + epsilon)
        for b in range(NX * NZ):
            z, x = divmod(b, NX)
            src = slice(b * OWN, (b + 1) * OWN)
            part = raw_ref[c, :, src].astype(jnp.float32) * scale * gain_ref[:, src]
            done_ref[c, x, :, z * OWN : (z + 1) * OWN] = part.astype(jnp.bfloat16)
        for x in range(NX):
            dst = out_ref.at[x, 0, pl.ds(c * ROWS, ROWS)]
            stores.append(pltpu.make_async_copy(done_ref.at[c, x], dst, out_sem.at[c, x]))
            stores[-1].start()
    for copy in moves + stores:
        copy.wait()


def prep(tokens, gain, upstream):
    return pl.pallas_call(
        prep_kernel,
        in_specs=[
            pl.BlockSpec(memory_space=pl.ANY),
            pl.BlockSpec(memory_space=pltpu.VMEM),
            pl.BlockSpec(memory_space=pl.ANY),
        ],
        out_specs=pl.BlockSpec(memory_space=pl.ANY),
        out_shape=jax.ShapeDtypeStruct((NX, 2, TOK, FEAT), jnp.bfloat16),
        scratch_shapes=[
            pltpu.VMEM((CHUNKS, ROWS, D), jnp.bfloat16),
            pltpu.VMEM((CHUNKS, NX, ROWS, FEAT), jnp.bfloat16),
            pltpu.SemaphoreType.DMA((CHUNKS,)),
            pltpu.SemaphoreType.DMA((CHUNKS, NX)),
            pltpu.SemaphoreType.DMA((NX * NZ,)),
        ],
        compiler_params=pltpu.CompilerParams(vmem_limit_bytes=DIRECT_LIMIT),
        cost_estimate=pl.CostEstimate(
            flops=6 * TOK * D, bytes_accessed=8 * TOK * D, transcendentals=0
        ),
    )(tokens, gain, upstream)


def project_kernel(feat_ref, *refs):
    low_refs, out_ref, low_ref = refs[:QUAD], refs[QUAD], refs[QUAD + 1]
    me = lax.axis_index("z")

    @pl.when(pl.program_id(0) == 0)
    def _():
        for near in range(QUAD):
            for far in range(2):
                at = pl.multiple_of((me ^ (near + QUAD * far)) * OWN, OWN)
                low_ref[:, pl.ds(at, OWN)] = low_refs[near][far]

    for s in range(2):
        for half in range(2):
            rows = slice(half * R, (half + 1) * R)
            part = lax.dot_general(
                low_ref[rows], feat_ref[s, half], LAST, preferred_element_type=jnp.float32
            )
            for x in range(NX):
                out_ref[x, s, rows] = part


def project(feat, lows):
    return pl.pallas_call(
        project_kernel,
        grid=(NX // 2,),
        in_specs=[pl.BlockSpec((2, 2, TOK, FEAT), lambda i: (i, 0, 0, 0))]
        + [pl.BlockSpec((2, 2 * R, OWN), lambda i: (0, 0, 0)) for _ in lows],
        out_specs=pl.BlockSpec((NX, 2, 2 * R, TOK), lambda i: (0, i, 0, 0)),
        out_shape=jax.ShapeDtypeStruct((NX, NX, 2 * R, TOK), jnp.float32),
        scratch_shapes=[pltpu.VMEM((2 * R, FEAT), jnp.bfloat16)],
        compiler_params=pltpu.CompilerParams(vmem_limit_bytes=VMEM_LIMIT),
        cost_estimate=pl.CostEstimate(
            flops=4 * NX * TOK * FEAT * R, bytes_accessed=6 * 1024 * 1024, transcendentals=0
        ),
    )(feat, *lows)


def grads_kernel(part_ref, feat_ref, out_ref, low_ref):
    step = pl.program_id(0)

    @pl.when(step == 0)
    def _():
        for s in range(NX):
            total = part_ref[0, s]
            for x in range(1, NX):
                total = total + part_ref[x, s]
            at = slice(s * TOK, (s + 1) * TOK)
            low_ref[0, :, at] = (total[R:] * inv_rank).astype(jnp.bfloat16)
            low_ref[1, :, at] = (total[:R] * inv_width).astype(jnp.bfloat16)

    me = lax.axis_index("z")
    for half, scale in enumerate((inv_width, inv_rank)):
        rows = slice(half * R, (half + 1) * R)
        grad = jnp.dot(
            low_ref[half],
            feat_ref[:, half].reshape(NX * TOK, 2 * OWN),
            preferred_element_type=jnp.float32,
        )
        grad = (grad * scale).astype(jnp.bfloat16)
        for block in range(2):
            out_ref[me ^ (2 * step + block), rows] = grad[:, block * OWN : (block + 1) * OWN]


def grads(part, feat):
    return pl.pallas_call(
        grads_kernel,
        grid=(NZ // 2,),
        in_specs=[
            pl.BlockSpec(part.shape, lambda i: (0, 0, 0, 0)),
            pl.BlockSpec((NX, 2, TOK, 2 * OWN), lambda i: (0, 0, 0, i)),
        ],
        out_specs=pl.BlockSpec((NZ, 2 * R, OWN), lambda i: (0, 0, 0)),
        out_shape=jax.ShapeDtypeStruct((NZ, 2 * R, OWN), jnp.bfloat16),
        scratch_shapes=[pltpu.VMEM((2, R, NX * TOK), jnp.bfloat16)],
        compiler_params=pltpu.CompilerParams(vmem_limit_bytes=VMEM_LIMIT),
        cost_estimate=pl.CostEstimate(
            flops=4 * NX * TOK * FEAT * R, bytes_accessed=6 * 1024 * 1024, transcendentals=0
        ),
    )(part, feat)


def exchange(array, axis):
    return lax.all_to_all(array, axis, 0, 0, tiled=True)


def swapped(array, by):
    return lax.ppermute(array, "z", [(i, i ^ by) for i in range(NZ)])


def is_far(group):
    return group % (GROUPS // 2) in (0, GROUPS // 2 - 1)


def first_neighbour(array):
    return lax.ppermute(array, "blk", [(g, g ^ 1) for g in range(GROUPS)])


def second_neighbour(array):
    pairs = []
    for g in range(GROUPS):
        other = (g + 1 if g % 2 else g - 1) % GROUPS
        for z in range(NZ):
            pairs.append((g * NZ + z, other * NZ + (z ^ QUAD if is_far(g) else z)))
    return lax.ppermute(array, ("blk", "z"), pairs)


def local(tokens, norm_gain, adapt_in, adapt_out, upstream):
    wide, narrow = jnp.float32, jnp.bfloat16
    group = lax.axis_index("blk") % (GROUPS // 2)
    far = (group == 0) | (group == GROUPS // 2 - 1)

    feat = prep(tokens[0], norm_gain[None], upstream[0])
    feat, adapt_in, adapt_out = lax.optimization_barrier((feat, adapt_in, adapt_out))
    feat = exchange(feat, "x")

    master = jnp.concatenate([adapt_in[0].T, adapt_out[0].T], axis=0)
    opposite = swapped(master, QUAD)
    pair = jnp.stack([master, opposite]).astype(narrow)
    lows = [pair] + [swapped(pair, k) for k in range(1, QUAD)]
    base = second_neighbour(jnp.where(far, opposite, master)) + master + first_neighbour(master)
    feat, lows, base = lax.optimization_barrier((feat, lows, base))

    part = exchange(project(feat, lows), "x")
    pieces = grads(part, feat).reshape(2, QUAD, 2 * R, OWN)
    quad = pieces[:, 0].astype(wide)
    for k in range(1, QUAD):
        quad = quad + swapped(pieces[:, k], k).astype(wide)

    sent = quad.astype(narrow)
    second = second_neighbour(sent).astype(wide)
    second = jnp.where(far, second[::-1], second)
    around = quad + first_neighbour(sent).astype(wide) + second
    total = around[0] + swapped(around[1].astype(narrow), QUAD).astype(wide)
    mixed = (base - step_size * total) / 3.0
    return (mixed[:R].T[None], mixed[R:].T[None])


def solution(mesh):
    mesh = Mesh(mesh.devices.reshape(GROUPS, NZ, NX), ("blk", "z", "x"))
    split = P("blk", ("z", "x"), None)
    in_specs = (split, P(), split, split, split)
    return jax.shard_map(
        local, mesh=mesh, in_specs=in_specs, out_specs=(split, split), check_vma=False
    )
```

```python
import jax
import jax.numpy as jnp
from jax import lax
from jax.experimental import pallas as pl
from jax.experimental.pallas import tpu as pltpu
from jax.sharding import Mesh
from jax.sharding import PartitionSpec as P

D = 8192
R = 64
TOKENS = 4096
GROUPS = 16
NX = 4
NZ = 8
TOK = TOKENS // (NX * NZ)
OWN = D // (NX * NZ)
QUAD = NZ // 2
FEAT = D // NX

learning_rate = 4.0
epsilon = 1e-05

inv_width = D ** (-0.5)
inv_rank = R ** (-0.5)
step_size = learning_rate / TOKENS**0.5

ROWS = 32
CHUNKS = TOK // ROWS

LAST = (((1,), (1,)), ((), ()))
VMEM_LIMIT = 40 * 1024 * 1024
DIRECT_LIMIT = 60 * 1024 * 1024


def prep_kernel(tok_ref, gain_ref, up_ref, out_ref, raw_ref, done_ref, in_sem, out_sem):
    sources = (up_ref, tok_ref)
    loads = {}
    for c in range(CHUNKS):
        rows = pl.ds(c * ROWS, ROWS)
        for h in range(2):
            loads[c, h] = pltpu.make_async_copy(
                sources[h].at[rows], raw_ref.at[c, h], in_sem.at[c, h]
            )
            loads[c, h].start()
    stores = []
    for c in range(CHUNKS):
        rows = pl.ds(c * ROWS, ROWS)
        for h in range(2):
            loads[c, h].wait()
            if h == 1:
                wide = raw_ref[c, h].astype(jnp.float32)
                scale = lax.rsqrt(jnp.mean(wide * wide, axis=-1, keepdims=True) + epsilon)
            for x in range(NX):
                for z in range(NZ):
                    at = slice((z * NX + x) * OWN, (z * NX + x + 1) * OWN)
                    part = raw_ref[c, h, :, at]
                    if h == 1:
                        part = part.astype(jnp.float32) * scale * gain_ref[:, at]
                    part = part.astype(jnp.bfloat16)
                    done_ref[c, x, h, :, z * OWN : (z + 1) * OWN] = part
                dst = out_ref.at[x, h, rows]
                stores.append(
                    pltpu.make_async_copy(done_ref.at[c, x, h], dst, out_sem.at[c, x, h])
                )
                stores[-1].start()
    for copy in stores:
        copy.wait()


def prep(tokens, gain, upstream):
    return pl.pallas_call(
        prep_kernel,
        in_specs=[
            pl.BlockSpec(memory_space=pl.ANY),
            pl.BlockSpec(memory_space=pltpu.VMEM),
            pl.BlockSpec(memory_space=pl.ANY),
        ],
        out_specs=pl.BlockSpec(memory_space=pl.ANY),
        out_shape=jax.ShapeDtypeStruct((NX, 2, TOK, FEAT), jnp.bfloat16),
        scratch_shapes=[
            pltpu.VMEM((CHUNKS, 2, ROWS, D), jnp.bfloat16),
            pltpu.VMEM((CHUNKS, NX, 2, ROWS, FEAT), jnp.bfloat16),
            pltpu.SemaphoreType.DMA((CHUNKS, 2)),
            pltpu.SemaphoreType.DMA((CHUNKS, NX, 2)),
        ],
        compiler_params=pltpu.CompilerParams(vmem_limit_bytes=DIRECT_LIMIT),
        cost_estimate=pl.CostEstimate(
            flops=6 * TOK * D, bytes_accessed=8 * TOK * D, transcendentals=0
        ),
    )(tokens, gain, upstream)


def project_kernel(feat_ref, *refs):
    low_refs, out_ref, low_ref = refs[:QUAD], refs[QUAD], refs[QUAD + 1]
    me = lax.axis_index("z")

    @pl.when(pl.program_id(0) == 0)
    def _():
        for near in range(QUAD):
            for far in range(2):
                at = pl.multiple_of((me ^ (near + QUAD * far)) * OWN, OWN)
                low_ref[:, pl.ds(at, OWN)] = low_refs[near][far]

    for s in range(2):
        for half in range(2):
            rows = slice(half * R, (half + 1) * R)
            part = lax.dot_general(
                low_ref[rows], feat_ref[s, 1 - half], LAST, preferred_element_type=jnp.float32
            )
            for x in range(NX):
                out_ref[x, s, rows] = part


def project(feat, lows):
    return pl.pallas_call(
        project_kernel,
        grid=(NX // 2,),
        in_specs=[pl.BlockSpec((2, 2, TOK, FEAT), lambda i: (i, 0, 0, 0))]
        + [pl.BlockSpec((2, 2 * R, OWN), lambda i: (0, 0, 0)) for _ in lows],
        out_specs=pl.BlockSpec((NX, 2, 2 * R, TOK), lambda i: (0, i, 0, 0)),
        out_shape=jax.ShapeDtypeStruct((NX, NX, 2 * R, TOK), jnp.float32),
        scratch_shapes=[pltpu.VMEM((2 * R, FEAT), jnp.bfloat16)],
        compiler_params=pltpu.CompilerParams(vmem_limit_bytes=VMEM_LIMIT),
        cost_estimate=pl.CostEstimate(
            flops=4 * NX * TOK * FEAT * R, bytes_accessed=6 * 1024 * 1024, transcendentals=0
        ),
    )(feat, *lows)


def grads_kernel(part_ref, feat_ref, out_ref, low_ref):
    step = pl.program_id(0)

    @pl.when(step == 0)
    def _():
        for s in range(NX):
            total = part_ref[0, s]
            for x in range(1, NX):
                total = total + part_ref[x, s]
            at = slice(s * TOK, (s + 1) * TOK)
            low_ref[0, :, at] = (total[R:] * inv_rank).astype(jnp.bfloat16)
            low_ref[1, :, at] = (total[:R] * inv_width).astype(jnp.bfloat16)

    me = lax.axis_index("z")
    for half, scale in enumerate((inv_width, inv_rank)):
        rows = slice(half * R, (half + 1) * R)
        grad = jnp.dot(
            low_ref[half],
            feat_ref[:, 1 - half].reshape(NX * TOK, 2 * OWN),
            preferred_element_type=jnp.float32,
        )
        grad = (grad * scale).astype(jnp.bfloat16)
        for block in range(2):
            out_ref[me ^ (2 * step + block), rows] = grad[:, block * OWN : (block + 1) * OWN]


def grads(part, feat):
    return pl.pallas_call(
        grads_kernel,
        grid=(NZ // 2,),
        in_specs=[
            pl.BlockSpec(part.shape, lambda i: (0, 0, 0, 0)),
            pl.BlockSpec((NX, 2, TOK, 2 * OWN), lambda i: (0, 0, 0, i)),
        ],
        out_specs=pl.BlockSpec((NZ, 2 * R, OWN), lambda i: (0, 0, 0)),
        out_shape=jax.ShapeDtypeStruct((NZ, 2 * R, OWN), jnp.bfloat16),
        scratch_shapes=[pltpu.VMEM((2, R, NX * TOK), jnp.bfloat16)],
        compiler_params=pltpu.CompilerParams(vmem_limit_bytes=VMEM_LIMIT),
        cost_estimate=pl.CostEstimate(
            flops=4 * NX * TOK * FEAT * R, bytes_accessed=6 * 1024 * 1024, transcendentals=0
        ),
    )(part, feat)


def exchange(array, axis):
    return lax.all_to_all(array, axis, 0, 0, tiled=True)


def swapped(array, by):
    return lax.ppermute(array, "z", [(i, i ^ by) for i in range(NZ)])


def is_far(group):
    return group % (GROUPS // 2) in (0, GROUPS // 2 - 1)


def first_neighbour(array):
    return lax.ppermute(array, "blk", [(g, g ^ 1) for g in range(GROUPS)])


def second_neighbour(array):
    pairs = []
    for g in range(GROUPS):
        other = (g + 1 if g % 2 else g - 1) % GROUPS
        for z in range(NZ):
            pairs.append((g * NZ + z, other * NZ + (z ^ QUAD if is_far(g) else z)))
    return lax.ppermute(array, ("blk", "z"), pairs)


def local(tokens, norm_gain, adapt_in, adapt_out, upstream):
    wide, narrow = jnp.float32, jnp.bfloat16
    far = ((lax.axis_index("blk") + 1) & (GROUPS // 2 - 1)) < 2

    feat = prep(tokens[0], norm_gain[None], upstream[0])
    feat, adapt_in, adapt_out = lax.optimization_barrier((feat, adapt_in, adapt_out))
    feat = exchange(feat, "x")

    master = jnp.concatenate([adapt_in[0].T, adapt_out[0].T], axis=0)
    opposite = swapped(master, QUAD)
    pair = jnp.stack([master, opposite]).astype(narrow)
    lows = [pair] + [swapped(pair, k) for k in range(1, QUAD)]
    base = second_neighbour(jnp.where(far, opposite, master)) + master + first_neighbour(master)
    feat, lows, base = lax.optimization_barrier((feat, lows, base))

    part = exchange(project(feat, lows), "x")
    pieces = grads(part, feat).reshape(2, QUAD, 2 * R, OWN)
    quad = pieces[:, 0].astype(wide)
    for k in range(1, QUAD):
        quad = quad + swapped(pieces[:, k], k).astype(wide)

    sent = quad.astype(narrow)
    second = second_neighbour(sent).astype(wide)
    second = jnp.where(far, second[::-1], second)
    around = quad + first_neighbour(sent).astype(wide) + second
    total = around[0] + swapped(around[1].astype(narrow), QUAD).astype(wide)
    mixed = (base - step_size * total) / 3.0
    return (mixed[:R].T[None], mixed[R:].T[None])


def solution(mesh):
    mesh = Mesh(mesh.devices.reshape(GROUPS, NZ, NX), ("blk", "z", "x"))
    split = P("blk", ("z", "x"), None)
    in_specs = (split, P(), split, split, split)
    return jax.shard_map(
        local, mesh=mesh, in_specs=in_specs, out_specs=(split, split), check_vma=False
    )
```

```python
import jax
import jax.numpy as jnp
from jax import lax
from jax.experimental import pallas as pl
from jax.experimental.pallas import tpu as pltpu
from jax.sharding import Mesh
from jax.sharding import PartitionSpec as P

D = 8192
R = 64
TOKENS = 4096
GROUPS = 16
NX = 4
NZ = 8
TOK = TOKENS // (NX * NZ)
OWN = D // (NX * NZ)
QUAD = NZ // 2
FEAT = D // NX

learning_rate = 4.0
epsilon = 1e-05

inv_width = D ** (-0.5)
inv_rank = R ** (-0.5)
step_size = learning_rate / TOKENS**0.5

ROWS = 32
CHUNKS = TOK // ROWS

LAST = (((1,), (1,)), ((), ()))
VMEM_LIMIT = 32 * 1024 * 1024
DIRECT_LIMIT = 60 * 1024 * 1024


def prep_kernel(tok_ref, gain_ref, up_ref, out_ref, raw_ref, done_ref, in_sem, out_sem):
    sources = (up_ref, tok_ref)
    loads = {}
    for c in range(CHUNKS):
        rows = pl.ds(c * ROWS, ROWS)
        for h in range(2):
            loads[c, h] = pltpu.make_async_copy(
                sources[h].at[rows], raw_ref.at[c, h], in_sem.at[c, h]
            )
            loads[c, h].start()
    stores = []
    for c in range(CHUNKS):
        rows = pl.ds(c * ROWS, ROWS)
        for h in range(2):
            loads[c, h].wait()
            if h == 1:
                wide = raw_ref[c, h].astype(jnp.float32)
                scale = lax.rsqrt(jnp.mean(wide * wide, axis=-1, keepdims=True) + epsilon)
            for x in range(NX):
                for z in range(NZ):
                    at = slice((z * NX + x) * OWN, (z * NX + x + 1) * OWN)
                    part = raw_ref[c, h, :, at]
                    if h == 1:
                        part = part.astype(jnp.float32) * scale * gain_ref[:, at]
                    part = part.astype(jnp.bfloat16)
                    done_ref[c, x, h, z] = part
                dst = out_ref.at[x, :, h, rows]
                stores.append(
                    pltpu.make_async_copy(done_ref.at[c, x, h], dst, out_sem.at[c, x, h])
                )
                stores[-1].start()
    for copy in stores:
        copy.wait()


def prep(tokens, gain, upstream):
    return pl.pallas_call(
        prep_kernel,
        in_specs=[
            pl.BlockSpec(memory_space=pl.ANY),
            pl.BlockSpec(memory_space=pltpu.VMEM),
            pl.BlockSpec(memory_space=pl.ANY),
        ],
        out_specs=pl.BlockSpec(memory_space=pl.ANY),
        out_shape=jax.ShapeDtypeStruct((NX, NZ, 2, TOK, OWN), jnp.bfloat16),
        scratch_shapes=[
            pltpu.VMEM((CHUNKS, 2, ROWS, D), jnp.bfloat16),
            pltpu.VMEM((CHUNKS, NX, 2, NZ, ROWS, OWN), jnp.bfloat16),
            pltpu.SemaphoreType.DMA((CHUNKS, 2)),
            pltpu.SemaphoreType.DMA((CHUNKS, NX, 2)),
        ],
        compiler_params=pltpu.CompilerParams(vmem_limit_bytes=DIRECT_LIMIT),
        cost_estimate=pl.CostEstimate(
            flops=6 * TOK * D, bytes_accessed=8 * TOK * D, transcendentals=0
        ),
    )(tokens, gain, upstream)


def project_kernel(feat_ref, *refs):
    low_refs, (out_ref, held_ref, low_ref, sem) = refs[:QUAD], refs[QUAD:]
    loads = []
    for s in range(NX):
        loads.append(pltpu.make_async_copy(feat_ref.at[s], held_ref.at[s], sem.at[s]))
        loads[-1].start()
    me = lax.axis_index("z")
    for near in range(QUAD):
        for far in range(2):
            low_ref[me ^ (near + QUAD * far)] = low_refs[near][far]
    for s in range(NX):
        loads[s].wait()
        for half in range(2):
            rows = slice(half * R, (half + 1) * R)
            part = jnp.zeros((R, TOK), jnp.float32)
            for z in range(NZ):
                part += lax.dot_general(
                    low_ref[z, rows],
                    held_ref[s, z, 1 - half],
                    LAST,
                    preferred_element_type=jnp.float32,
                )
            for x in range(NX):
                out_ref[x, s, rows] = part


def project(feat, lows):
    return pl.pallas_call(
        project_kernel,
        in_specs=[pl.BlockSpec(memory_space=pl.ANY)]
        + [pl.BlockSpec(memory_space=pltpu.VMEM) for _ in lows],
        out_specs=[pl.BlockSpec(memory_space=pltpu.VMEM) for _ in range(2)],
        out_shape=[jax.ShapeDtypeStruct((NX, NX, 2 * R, TOK), jnp.float32), feat],
        scratch_shapes=[
            pltpu.VMEM((NZ, 2 * R, OWN), jnp.bfloat16),
            pltpu.SemaphoreType.DMA((NX,)),
        ],
        compiler_params=pltpu.CompilerParams(vmem_limit_bytes=VMEM_LIMIT),
        cost_estimate=pl.CostEstimate(
            flops=4 * NX * TOK * FEAT * R, bytes_accessed=6 * 1024 * 1024, transcendentals=0
        ),
    )(feat, *lows)


def block_grad(low_ref, feat_ref, piece, half):
    block = feat_ref[:, lax.axis_index("z") ^ piece, 1 - half].reshape(NX * TOK, OWN)
    grad = jnp.dot(low_ref[half], block, preferred_element_type=jnp.float32)
    return grad * (inv_rank if half else inv_width)


SENT = [near + QUAD * far for near in range(1, QUAD) for far in range(2)]
KEPT = [0, QUAD]


def sent_kernel(part_ref, feat_ref, *refs):
    out_refs, low_ref = refs[: QUAD - 1], refs[QUAD - 1]
    for s in range(NX):
        total = part_ref[0, s]
        for x in range(1, NX):
            total = total + part_ref[x, s]
        at = slice(s * TOK, (s + 1) * TOK)
        low_ref[0, :, at] = (total[R:] * inv_rank).astype(jnp.bfloat16)
        low_ref[1, :, at] = (total[:R] * inv_width).astype(jnp.bfloat16)
    for piece in SENT:
        for half in range(2):
            rows = slice(half * R, (half + 1) * R)
            grad = block_grad(low_ref, feat_ref, piece, half).astype(jnp.bfloat16)
            out_refs[piece % QUAD - 1][piece // QUAD, rows] = grad


def kept_kernel(low_ref, feat_ref, out_ref):
    for i, piece in enumerate(KEPT):
        for half in range(2):
            out_ref[i, half * R : (half + 1) * R] = block_grad(low_ref, feat_ref, piece, half)


def grads(kernel, first, feat, pieces, outs):
    return pl.pallas_call(
        kernel,
        in_specs=[pl.BlockSpec(memory_space=pltpu.VMEM) for _ in range(2)],
        out_specs=[pl.BlockSpec(memory_space=pltpu.VMEM) for _ in outs],
        out_shape=outs,
        compiler_params=pltpu.CompilerParams(vmem_limit_bytes=VMEM_LIMIT),
        cost_estimate=pl.CostEstimate(
            flops=4 * NX * TOK * OWN * R * len(pieces),
            bytes_accessed=1024 * 1024 * len(pieces),
            transcendentals=0,
        ),
    )(first, feat)


def exchange(array, axis):
    return lax.all_to_all(array, axis, 0, 0, tiled=True)


def swapped(array, by):
    return lax.ppermute(array, "z", [(i, i ^ by) for i in range(NZ)])


def is_far(group):
    return group % (GROUPS // 2) in (0, GROUPS // 2 - 1)


def first_neighbour(array):
    return lax.ppermute(array, "blk", [(g, g ^ 1) for g in range(GROUPS)])


def second_neighbour(array):
    pairs = []
    for g in range(GROUPS):
        other = (g + 1 if g % 2 else g - 1) % GROUPS
        for z in range(NZ):
            pairs.append((g * NZ + z, other * NZ + (z ^ QUAD if is_far(g) else z)))
    return lax.ppermute(array, ("blk", "z"), pairs)


def local(tokens, norm_gain, adapt_in, adapt_out, upstream):
    wide, narrow = jnp.float32, jnp.bfloat16
    far = ((lax.axis_index("blk") + 1) & (GROUPS // 2 - 1)) < 2

    feat = prep(tokens[0], norm_gain[None], upstream[0])
    feat, adapt_in, adapt_out = lax.optimization_barrier((feat, adapt_in, adapt_out))
    feat = exchange(feat, "x")

    master = jnp.concatenate([adapt_in[0].T, adapt_out[0].T], axis=0)
    opposite = swapped(master, QUAD)
    pair = jnp.stack([master, opposite]).astype(narrow)
    lows = [pair] + [swapped(pair, k) for k in range(1, QUAD)]
    base = second_neighbour(jnp.where(far, opposite, master)) + master + first_neighbour(master)
    feat, lows, base = lax.optimization_barrier((feat, lows, base))

    part, feat = project(feat, lows)
    part = exchange(part, "x")
    piece = jax.ShapeDtypeStruct((2, 2 * R, OWN), narrow)
    lowered = jax.ShapeDtypeStruct((2, R, NX * TOK), narrow)
    *pieces, lowered = grads(sent_kernel, part, feat, SENT, [piece] * (QUAD - 1) + [lowered])
    pieces = [swapped(pieces[k - 1], k) for k in range(1, QUAD)]
    (quad,) = grads(kept_kernel, lowered, feat, KEPT, [jax.ShapeDtypeStruct(piece.shape, wide)])
    for got in pieces:
        quad = quad + got.astype(wide)

    sent = quad.astype(narrow)
    second = second_neighbour(sent).astype(wide)
    second = jnp.where(far, second[::-1], second)
    around = quad + first_neighbour(sent).astype(wide) + second
    total = around[0] + swapped(around[1].astype(narrow), QUAD).astype(wide)
    mixed_in = (base[:R] - step_size * total[:R]) / 3.0
    mixed_out = (base[R:] - step_size * total[R:]) / 3.0
    return (mixed_in.T[None], mixed_out.T[None])


def solution(mesh):
    mesh = Mesh(mesh.devices.reshape(GROUPS, NZ, NX), ("blk", "z", "x"))
    split = P("blk", ("z", "x"), None)
    in_specs = (split, P(), split, split, split)
    return jax.shard_map(
        local, mesh=mesh, in_specs=in_specs, out_specs=(split, split), check_vma=False
    )
```

```python
import jax
import jax.numpy as jnp
from jax import lax
from jax.experimental import pallas as pl
from jax.experimental.pallas import tpu as pltpu
from jax.sharding import Mesh
from jax.sharding import PartitionSpec as P

D = 8192
R = 64
TOKENS = 4096
GROUPS = 16
NX = 4
NZ = 8
TOK = TOKENS // (NX * NZ)
OWN = D // (NX * NZ)
QUAD = NZ // 2

learning_rate = 4.0
epsilon = 1e-05

inv_width = D ** (-0.5)
inv_rank = R ** (-0.5)
step_size = learning_rate / TOKENS**0.5

ROWS = 32
CHUNKS = TOK // ROWS

LAST = (((1,), (1,)), ((), ()))
VMEM_LIMIT = 32 * 1024 * 1024
DIRECT_LIMIT = 60 * 1024 * 1024


def prep_kernel(tok_ref, gain_ref, up_ref, keep_ref, send_ref, raw_ref, done_ref, in_sem, out_sem):
    sources = (up_ref, tok_ref)
    loads = {}
    for c in range(CHUNKS):
        rows = pl.ds(c * ROWS, ROWS)
        for h in range(2):
            loads[c, h] = pltpu.make_async_copy(
                sources[h].at[rows], raw_ref.at[c, h], in_sem.at[c, h]
            )
            loads[c, h].start()
    me = lax.axis_index("x")
    pair, mate = steps(lax.axis_index("blk"))
    columns = (me, me ^ mate, me ^ pair, me ^ pair ^ mate)
    stores = []
    for c in range(CHUNKS):
        rows = pl.ds(c * ROWS, ROWS)
        for h in range(2):
            loads[c, h].wait()
            if h == 1:
                wide = raw_ref[c, h].astype(jnp.float32)
                scale = lax.rsqrt(jnp.mean(wide * wide, axis=-1, keepdims=True) + epsilon)
            for i, column in enumerate(columns):
                for z in range(NZ):
                    at = pl.ds(pl.multiple_of((z * NX + column) * OWN, OWN), OWN)
                    part = raw_ref[c, h, :, at]
                    if h == 1:
                        part = part.astype(jnp.float32) * scale * gain_ref[:, at]
                    done_ref[c, h, i, z] = part.astype(jnp.bfloat16)
            for i, ref in enumerate((keep_ref, send_ref)):
                src = done_ref.at[c, h, pl.ds(2 * i, 2)]
                stores.append(
                    pltpu.make_async_copy(src, ref.at[:, :, h, rows], out_sem.at[c, h, i])
                )
                stores[-1].start()
    for copy in stores:
        copy.wait()


def prep(tokens, gain, upstream):
    out = jax.ShapeDtypeStruct((2, NZ, 2, TOK, OWN), jnp.bfloat16)
    return pl.pallas_call(
        prep_kernel,
        in_specs=[
            pl.BlockSpec(memory_space=pl.ANY),
            pl.BlockSpec(memory_space=pltpu.VMEM),
            pl.BlockSpec(memory_space=pl.ANY),
        ],
        out_specs=[pl.BlockSpec(memory_space=pl.ANY) for _ in range(2)],
        out_shape=[out, out],
        scratch_shapes=[
            pltpu.VMEM((CHUNKS, 2, ROWS, D), jnp.bfloat16),
            pltpu.VMEM((CHUNKS, 2, 4, NZ, ROWS, OWN), jnp.bfloat16),
            pltpu.SemaphoreType.DMA((CHUNKS, 2)),
            pltpu.SemaphoreType.DMA((CHUNKS, 2, 2)),
        ],
        compiler_params=pltpu.CompilerParams(vmem_limit_bytes=DIRECT_LIMIT),
        cost_estimate=pl.CostEstimate(
            flops=6 * TOK * D, bytes_accessed=8 * TOK * D, transcendentals=0
        ),
    )(tokens, gain, upstream)


def project_kernel(keep_ref, got_ref, *refs):
    piece_refs, (out_ref, held_ref, low_ref, sem) = refs[: 2 * QUAD], refs[2 * QUAD :]
    loads = []
    for t, ref in enumerate((keep_ref, got_ref)):
        loads.append(pltpu.make_async_copy(ref, held_ref.at[t], sem.at[t]))
        loads[-1].start()
    me = lax.axis_index("z")
    for c in range(2):
        for near in range(QUAD):
            for far in range(2):
                low_ref[c, me ^ (near + QUAD * far)] = piece_refs[QUAD * c + near][far]
    for t in range(2):
        loads[t].wait()
        for half in range(2):
            rows = slice(half * R, (half + 1) * R)
            part = jnp.zeros((R, TOK), jnp.float32)
            for c in range(2):
                for z in range(NZ):
                    part += lax.dot_general(
                        low_ref[c, z, rows],
                        held_ref[t, c, z, 1 - half],
                        LAST,
                        preferred_element_type=jnp.float32,
                    )
            out_ref[t, rows] = part


def project(keep, got, lows):
    return pl.pallas_call(
        project_kernel,
        in_specs=[pl.BlockSpec(memory_space=pl.ANY) for _ in range(2)]
        + [pl.BlockSpec(memory_space=pltpu.VMEM) for _ in lows],
        out_specs=[pl.BlockSpec(memory_space=pltpu.VMEM) for _ in range(2)],
        out_shape=[
            jax.ShapeDtypeStruct((2, 2 * R, TOK), jnp.float32),
            jax.ShapeDtypeStruct((2,) + keep.shape, keep.dtype),
        ],
        scratch_shapes=[
            pltpu.VMEM((2, NZ, 2 * R, OWN), jnp.bfloat16),
            pltpu.SemaphoreType.DMA((2,)),
        ],
        compiler_params=pltpu.CompilerParams(vmem_limit_bytes=VMEM_LIMIT),
        cost_estimate=pl.CostEstimate(
            flops=8 * TOK * D * R, bytes_accessed=6 * 1024 * 1024, transcendentals=0
        ),
    )(keep, got, *lows)


EARLY, LATE = (3, 2), (1, 0)


def column_grads(low_ref, feat_ref, out_refs, column):
    me = lax.axis_index("z")
    for nears, out_ref in zip((EARLY, LATE), out_refs, strict=True):
        for i, near in enumerate(nears):
            for far in range(2):
                for half, scale in enumerate((inv_width, inv_rank)):
                    block = feat_ref[:, column, me ^ (near + QUAD * far), 1 - half]
                    block = block.reshape(2 * TOK, OWN)
                    grad = jnp.dot(low_ref[half], block, preferred_element_type=jnp.float32)
                    rows = slice(half * R, (half + 1) * R)
                    out_ref[i, far, rows] = (grad * scale).astype(out_ref.dtype)


def other_kernel(part_ref, got_ref, feat_ref, early_ref, late_ref, low_ref):
    for t in range(2):
        total = part_ref[t] + got_ref[1 - t]
        at = slice(t * TOK, (t + 1) * TOK)
        low_ref[0, :, at] = (total[R:] * inv_rank).astype(jnp.bfloat16)
        low_ref[1, :, at] = (total[:R] * inv_width).astype(jnp.bfloat16)
    column_grads(low_ref, feat_ref, (early_ref, late_ref), 1)


def own_kernel(low_ref, feat_ref, early_ref, late_ref):
    column_grads(low_ref, feat_ref, (early_ref, late_ref), 0)


def early_kernel(own_ref, got_ref, first_ref, second_ref):
    for i, ref in enumerate((first_ref, second_ref)):
        ref[...] = (own_ref[i] + got_ref[i].astype(jnp.float32)).astype(ref.dtype)


def late_kernel(master_ref, own_ref, got_ref, sent_ref, kept_ref):
    sent_ref[...] = (own_ref[0] + got_ref[0].astype(jnp.float32)).astype(sent_ref.dtype)
    kept_ref[0] = own_ref[1, 0] + got_ref[1, 0].astype(jnp.float32) - master_ref[...] / step_size
    kept_ref[1] = own_ref[1, 1] + got_ref[1, 1].astype(jnp.float32)


def small(kernel, outs, *args):
    return pl.pallas_call(
        kernel,
        in_specs=[pl.BlockSpec(memory_space=pltpu.VMEM) for _ in args],
        out_specs=[pl.BlockSpec(memory_space=pltpu.VMEM) for _ in outs],
        out_shape=outs,
        compiler_params=pltpu.CompilerParams(vmem_limit_bytes=VMEM_LIMIT),
        cost_estimate=pl.CostEstimate(
            flops=2 * TOK * D * R, bytes_accessed=1024 * 1024, transcendentals=0
        ),
    )(*args)


def steps(group):
    odd = group % 2
    return 1 + 2 * odd, 3 - 2 * odd


def along_x(array, which):
    pairs = []
    for g in range(GROUPS):
        for x in range(NX):
            pairs.append((g * NX + x, g * NX + (x ^ steps(g)[which])))
    return lax.ppermute(array, ("blk", "x"), pairs)


def swapped(array, by):
    return lax.ppermute(array, "z", [(i, i ^ by) for i in range(NZ)])


def is_far(group):
    return group % (GROUPS // 2) in (0, GROUPS // 2 - 1)


def first_neighbour(array):
    return lax.ppermute(array, "blk", [(g, g ^ 1) for g in range(GROUPS)])


def second_neighbour(array):
    pairs = []
    for g in range(GROUPS):
        other = (g + 1 if g % 2 else g - 1) % GROUPS
        for z in range(NZ):
            pairs.append((g * NZ + z, other * NZ + (z ^ QUAD if is_far(g) else z)))
    return lax.ppermute(array, ("blk", "z"), pairs)


def local(tokens, norm_gain, adapt_in, adapt_out, upstream):
    wide, narrow = jnp.float32, jnp.bfloat16
    far = ((lax.axis_index("blk") + 1) & (GROUPS // 2 - 1)) < 2

    master = jnp.concatenate([adapt_in[0].T, adapt_out[0].T], axis=0)
    own = master.astype(narrow)
    pair = jnp.stack([own, swapped(own, QUAD)])
    lows = [pair] + [swapped(pair, k) for k in range(1, QUAD)]
    lows += [along_x(low, 1) for low in lows]

    keep, send = prep(tokens[0], norm_gain[None], upstream[0])
    got = along_x(send, 0)
    part, feat = project(keep, got, lows)
    part_got = along_x(part, 0)

    narrow_pieces = jax.ShapeDtypeStruct((2, 2, 2 * R, OWN), narrow)
    wide_pieces = jax.ShapeDtypeStruct(narrow_pieces.shape, wide)
    lowered = jax.ShapeDtypeStruct((2, R, 2 * TOK), narrow)
    *theirs, lowered = small(
        other_kernel, [narrow_pieces, narrow_pieces, lowered], part, part_got, feat
    )
    theirs = [along_x(pieces, 1) for pieces in theirs]
    mine = small(own_kernel, [wide_pieces, wide_pieces], lowered, feat)
    piece = jax.ShapeDtypeStruct((2, 2 * R, OWN), narrow)
    kept = jax.ShapeDtypeStruct(piece.shape, wide)
    sent = small(early_kernel, [piece, piece], mine[0], theirs[0])
    early = [swapped(array, near) for array, near in zip(sent, EARLY, strict=True)]
    sent, quad = small(late_kernel, [piece, kept], master, mine[1], theirs[1])
    for got in early + [swapped(sent, LATE[0])]:
        quad = quad + got.astype(wide)

    sent = quad.astype(narrow)
    second = second_neighbour(sent).astype(wide)
    second = jnp.where(far, second[::-1], second)
    around = quad + first_neighbour(sent).astype(wide) + second
    total = around[0] + swapped(around[1].astype(narrow), QUAD).astype(wide)
    mixed = [total[half * R : (half + 1) * R] * (-step_size / 3.0) for half in range(2)]
    return (mixed[0].T[None], mixed[1].T[None])


def solution(mesh):
    mesh = Mesh(mesh.devices.reshape(GROUPS, NZ, NX), ("blk", "z", "x"))
    split = P("blk", ("z", "x"), None)
    in_specs = (split, P(), split, split, split)
    return jax.shard_map(
        local, mesh=mesh, in_specs=in_specs, out_specs=(split, split), check_vma=False
    )
```

```python
import jax
import jax.numpy as jnp
from jax import lax
from jax.experimental import pallas as pl
from jax.experimental.pallas import tpu as pltpu
from jax.sharding import Mesh
from jax.sharding import PartitionSpec as P

D = 8192
R = 64
TOKENS = 4096
GROUPS = 16
NX = 4
NZ = 8
TOK = TOKENS // (NX * NZ)
OWN = D // (NX * NZ)
QUAD = NZ // 2

learning_rate = 4.0
epsilon = 1e-05

inv_width = D ** (-0.5)
inv_rank = R ** (-0.5)
step_size = learning_rate / TOKENS**0.5

ROWS = 32
CHUNKS = TOK // ROWS

LAST = (((1,), (1,)), ((), ()))
VMEM_LIMIT = 32 * 1024 * 1024
DIRECT_LIMIT = 60 * 1024 * 1024


def prep_kernel(tok_ref, gain_ref, up_ref, keep_ref, send_ref, raw_ref, done_ref, in_sem, out_sem):
    sources = (up_ref, tok_ref)
    loads = {}
    for c in range(CHUNKS):
        rows = pl.ds(c * ROWS, ROWS)
        for h in range(2):
            loads[c, h] = pltpu.make_async_copy(
                sources[h].at[rows], raw_ref.at[c, h], in_sem.at[c, h]
            )
            loads[c, h].start()
    me = lax.axis_index("x")
    pair, mate = steps(lax.axis_index("blk"))
    columns = (me, me ^ mate, me ^ pair, me ^ pair ^ mate)
    stores = []
    for c in range(CHUNKS):
        rows = pl.ds(c * ROWS, ROWS)
        for h in range(2):
            loads[c, h].wait()
            if h == 1:
                wide = raw_ref[c, h].astype(jnp.float32)
                scale = lax.rsqrt(jnp.mean(wide * wide, axis=-1, keepdims=True) + epsilon)
            for i, column in enumerate(columns):
                for z in range(NZ):
                    at = pl.ds(pl.multiple_of((z * NX + column) * OWN, OWN), OWN)
                    part = raw_ref[c, h, :, at]
                    if h == 1:
                        part = part.astype(jnp.float32) * scale * gain_ref[:, at]
                    done_ref[c, h, i, z] = part.astype(jnp.bfloat16)
            for i, ref in enumerate((keep_ref, send_ref)):
                src = done_ref.at[c, h, pl.ds(2 * i, 2)]
                stores.append(
                    pltpu.make_async_copy(src, ref.at[:, :, h, rows], out_sem.at[c, h, i])
                )
                stores[-1].start()
    for copy in stores:
        copy.wait()


def prep(tokens, gain, upstream):
    out = jax.ShapeDtypeStruct((2, NZ, 2, TOK, OWN), jnp.bfloat16)
    return pl.pallas_call(
        prep_kernel,
        in_specs=[
            pl.BlockSpec(memory_space=pl.ANY),
            pl.BlockSpec(memory_space=pltpu.VMEM),
            pl.BlockSpec(memory_space=pl.ANY),
        ],
        out_specs=[pl.BlockSpec(memory_space=pl.ANY) for _ in range(2)],
        out_shape=[out, out],
        scratch_shapes=[
            pltpu.VMEM((CHUNKS, 2, ROWS, D), jnp.bfloat16),
            pltpu.VMEM((CHUNKS, 2, 4, NZ, ROWS, OWN), jnp.bfloat16),
            pltpu.SemaphoreType.DMA((CHUNKS, 2)),
            pltpu.SemaphoreType.DMA((CHUNKS, 2, 2)),
        ],
        compiler_params=pltpu.CompilerParams(vmem_limit_bytes=DIRECT_LIMIT),
        cost_estimate=pl.CostEstimate(
            flops=6 * TOK * D, bytes_accessed=8 * TOK * D, transcendentals=0
        ),
    )(tokens, gain, upstream)


def project_kernel(keep_ref, got_ref, *refs):
    piece_refs, (out_ref, held_ref, low_ref, sem) = refs[:2], refs[2:]
    loads = []
    for t, ref in enumerate((keep_ref, got_ref)):
        loads.append(pltpu.make_async_copy(ref, held_ref.at[t], sem.at[t]))
        loads[-1].start()
    half = lax.axis_index("half")
    for c, ref in enumerate(piece_refs):
        for near in range(QUAD):
            for far in range(2):
                low_ref[c, QUAD * (half ^ far) + near] = ref[near, far]
    for t in range(2):
        loads[t].wait()
        for half in range(2):
            rows = slice(half * R, (half + 1) * R)
            part = jnp.zeros((R, TOK), jnp.float32)
            for c in range(2):
                for z in range(NZ):
                    part += lax.dot_general(
                        low_ref[c, z, rows],
                        held_ref[t, c, z, 1 - half],
                        LAST,
                        preferred_element_type=jnp.float32,
                    )
            out_ref[t, rows] = part


def project(keep, got, lows):
    return pl.pallas_call(
        project_kernel,
        in_specs=[pl.BlockSpec(memory_space=pl.ANY) for _ in range(2)]
        + [pl.BlockSpec(memory_space=pltpu.VMEM) for _ in lows],
        out_specs=[pl.BlockSpec(memory_space=pltpu.VMEM) for _ in range(2)],
        out_shape=[
            jax.ShapeDtypeStruct((2, 2 * R, TOK), jnp.float32),
            jax.ShapeDtypeStruct((2,) + keep.shape, keep.dtype),
        ],
        scratch_shapes=[
            pltpu.VMEM((2, NZ, 2 * R, OWN), jnp.bfloat16),
            pltpu.SemaphoreType.DMA((2,)),
        ],
        compiler_params=pltpu.CompilerParams(vmem_limit_bytes=VMEM_LIMIT),
        cost_estimate=pl.CostEstimate(
            flops=8 * TOK * D * R, bytes_accessed=6 * 1024 * 1024, transcendentals=0
        ),
    )(keep, got, *lows)


EARLY, LATE = (3, 2), (1, 0)


def column_grads(low_ref, feat_ref, out_refs, column):
    me = my_z()
    for nears, out_ref in zip((EARLY, LATE), out_refs, strict=True):
        for i, near in enumerate(nears):
            for far in range(2):
                for half, scale in enumerate((inv_width, inv_rank)):
                    block = feat_ref[:, column, me ^ (near + QUAD * far), 1 - half]
                    block = block.reshape(2 * TOK, OWN)
                    grad = jnp.dot(low_ref[half], block, preferred_element_type=jnp.float32)
                    rows = slice(half * R, (half + 1) * R)
                    out_ref[i, far, rows] = (grad * scale).astype(out_ref.dtype)


def other_kernel(part_ref, got_ref, feat_ref, early_ref, late_ref, low_ref):
    for t in range(2):
        total = part_ref[t] + got_ref[1 - t]
        at = slice(t * TOK, (t + 1) * TOK)
        low_ref[0, :, at] = (total[R:] * inv_rank).astype(jnp.bfloat16)
        low_ref[1, :, at] = (total[:R] * inv_width).astype(jnp.bfloat16)
    column_grads(low_ref, feat_ref, (early_ref, late_ref), 1)


def own_kernel(low_ref, feat_ref, early_ref, late_ref):
    column_grads(low_ref, feat_ref, (early_ref, late_ref), 0)


def early_kernel(own_ref, got_ref, first_ref, second_ref):
    for i, ref in enumerate((first_ref, second_ref)):
        ref[...] = (own_ref[i] + got_ref[i].astype(jnp.float32)).astype(ref.dtype)


def late_kernel(master_ref, own_ref, got_ref, sent_ref, kept_ref):
    sent_ref[...] = (own_ref[0] + got_ref[0].astype(jnp.float32)).astype(sent_ref.dtype)
    kept_ref[0] = own_ref[1, 0] + got_ref[1, 0].astype(jnp.float32) - master_ref[...] / step_size
    kept_ref[1] = own_ref[1, 1] + got_ref[1, 1].astype(jnp.float32)


def small(kernel, outs, *args):
    return pl.pallas_call(
        kernel,
        in_specs=[pl.BlockSpec(memory_space=pltpu.VMEM) for _ in args],
        out_specs=[pl.BlockSpec(memory_space=pltpu.VMEM) for _ in outs],
        out_shape=outs,
        compiler_params=pltpu.CompilerParams(vmem_limit_bytes=VMEM_LIMIT),
        cost_estimate=pl.CostEstimate(
            flops=2 * TOK * D * R, bytes_accessed=1024 * 1024, transcendentals=0
        ),
    )(*args)


def steps(group):
    odd = group % 2
    return 1 + 2 * odd, 3 - 2 * odd


def along_x(array, which):
    pairs = []
    for g in range(GROUPS):
        for x in range(NX):
            pairs.append((g * NX + x, g * NX + (x ^ steps(g)[which])))
    return lax.ppermute(array, ("blk", "x"), pairs)


def swapped(array, by):
    return lax.ppermute(array, ("half", "near"), [(i, i ^ by) for i in range(NZ)])


def my_z():
    return QUAD * lax.axis_index("half") + lax.axis_index("near")


def is_far(group):
    return group % (GROUPS // 2) in (0, GROUPS // 2 - 1)


def first_neighbour(array):
    return lax.ppermute(array, "blk", [(g, g ^ 1) for g in range(GROUPS)])


def second_neighbour(array):
    pairs = []
    for g in range(GROUPS):
        other = (g + 1 if g % 2 else g - 1) % GROUPS
        for z in range(NZ):
            pairs.append((g * NZ + z, other * NZ + (z ^ QUAD if is_far(g) else z)))
    return lax.ppermute(array, ("blk", "half", "near"), pairs)


def local(tokens, norm_gain, adapt_in, adapt_out, upstream):
    wide, narrow = jnp.float32, jnp.bfloat16
    far = ((lax.axis_index("blk") + 1) & (GROUPS // 2 - 1)) < 2

    master = jnp.concatenate([adapt_in[0].T, adapt_out[0].T], axis=0)
    own = master.astype(narrow)
    pair = jnp.stack([own, swapped(own, QUAD)])
    low = lax.all_to_all(jnp.broadcast_to(pair, (QUAD,) + pair.shape), "near", 0, 0, tiled=True)
    lows = [low, along_x(low, 1)]

    keep, send = prep(tokens[0], norm_gain[None], upstream[0])
    got = along_x(send, 0)
    part, feat = project(keep, got, lows)
    part_got = along_x(part, 0)

    narrow_pieces = jax.ShapeDtypeStruct((2, 2, 2 * R, OWN), narrow)
    wide_pieces = jax.ShapeDtypeStruct(narrow_pieces.shape, wide)
    lowered = jax.ShapeDtypeStruct((2, R, 2 * TOK), narrow)
    *theirs, lowered = small(
        other_kernel, [narrow_pieces, narrow_pieces, lowered], part, part_got, feat
    )
    theirs = [along_x(pieces, 1) for pieces in theirs]
    mine = small(own_kernel, [wide_pieces, wide_pieces], lowered, feat)
    piece = jax.ShapeDtypeStruct((2, 2 * R, OWN), narrow)
    kept = jax.ShapeDtypeStruct(piece.shape, wide)
    sent = small(early_kernel, [piece, piece], mine[0], theirs[0])
    early = [swapped(array, near) for array, near in zip(sent, EARLY, strict=True)]
    sent, quad = small(late_kernel, [piece, kept], master, mine[1], theirs[1])
    for got in early + [swapped(sent, LATE[0])]:
        quad = quad + got.astype(wide)

    sent = quad.astype(narrow)
    second = second_neighbour(sent).astype(wide)
    second = jnp.where(far, second[::-1], second)
    around = quad + first_neighbour(sent).astype(wide) + second
    total = around[0] + swapped(around[1].astype(narrow), QUAD).astype(wide)
    mixed = [total[half * R : (half + 1) * R] * (-step_size / 3.0) for half in range(2)]
    return (mixed[0].T[None], mixed[1].T[None])


def solution(mesh):
    axes = ("blk", "half", "near", "x")
    mesh = Mesh(mesh.devices.reshape(GROUPS, 2, QUAD, NX), axes)
    split = P("blk", axes[1:], None)
    in_specs = (split, P(), split, split, split)
    return jax.shard_map(
        local, mesh=mesh, in_specs=in_specs, out_specs=(split, split), check_vma=False
    )
```

```python
import jax
import jax.numpy as jnp
from jax import lax
from jax.experimental import pallas as pl
from jax.experimental.pallas import tpu as pltpu
from jax.sharding import Mesh
from jax.sharding import PartitionSpec as P

D = 8192
R = 64
TOKENS = 4096
GROUPS = 16
NX = 4
NZ = 8
TOK = TOKENS // (NX * NZ)
OWN = D // (NX * NZ)
QUAD = NZ // 2

learning_rate = 4.0
epsilon = 1e-05

inv_width = D ** (-0.5)
inv_rank = R ** (-0.5)
step_size = learning_rate / TOKENS**0.5

ROWS = 32
CHUNKS = TOK // ROWS

LAST = (((1,), (1,)), ((), ()))
VMEM_LIMIT = 32 * 1024 * 1024
DIRECT_LIMIT = 60 * 1024 * 1024


def prep_kernel(tok_ref, gain_ref, up_ref, keep_ref, send_ref, raw_ref, done_ref, in_sem, out_sem):
    sources = (up_ref, tok_ref)
    loads = {}
    for c in range(CHUNKS):
        rows = pl.ds(c * ROWS, ROWS)
        for h in range(2):
            loads[c, h] = pltpu.make_async_copy(
                sources[h].at[rows], raw_ref.at[c, h], in_sem.at[c, h]
            )
            loads[c, h].start()
    me = lax.axis_index("x")
    pair, mate = steps(lax.axis_index("blk"))
    columns = (me, me ^ mate, me ^ pair, me ^ pair ^ mate)
    stores = []
    for c in range(CHUNKS):
        rows = pl.ds(c * ROWS, ROWS)
        for h in range(2):
            loads[c, h].wait()
            if h == 1:
                wide = raw_ref[c, h].astype(jnp.float32)
                scale = lax.rsqrt(jnp.mean(wide * wide, axis=-1, keepdims=True) + epsilon)
            for i, column in enumerate(columns):
                for z in range(NZ):
                    at = pl.ds(pl.multiple_of((z * NX + column) * OWN, OWN), OWN)
                    part = raw_ref[c, h, :, at]
                    if h == 1:
                        part = part.astype(jnp.float32) * scale * gain_ref[:, at]
                    done_ref[c, h, i, z] = part.astype(jnp.bfloat16)
            for i, ref in enumerate((keep_ref, send_ref)):
                src = done_ref.at[c, h, pl.ds(2 * i, 2)]
                stores.append(
                    pltpu.make_async_copy(src, ref.at[:, :, h, rows], out_sem.at[c, h, i])
                )
                stores[-1].start()
    for copy in stores:
        copy.wait()


def prep(tokens, gain, upstream):
    out = jax.ShapeDtypeStruct((2, NZ, 2, TOK, OWN), jnp.bfloat16)
    return pl.pallas_call(
        prep_kernel,
        in_specs=[
            pl.BlockSpec(memory_space=pl.ANY),
            pl.BlockSpec(memory_space=pltpu.VMEM),
            pl.BlockSpec(memory_space=pl.ANY),
        ],
        out_specs=[pl.BlockSpec(memory_space=pl.ANY) for _ in range(2)],
        out_shape=[out, out],
        scratch_shapes=[
            pltpu.VMEM((CHUNKS, 2, ROWS, D), jnp.bfloat16),
            pltpu.VMEM((CHUNKS, 2, 4, NZ, ROWS, OWN), jnp.bfloat16),
            pltpu.SemaphoreType.DMA((CHUNKS, 2)),
            pltpu.SemaphoreType.DMA((CHUNKS, 2, 2)),
        ],
        compiler_params=pltpu.CompilerParams(vmem_limit_bytes=DIRECT_LIMIT),
        cost_estimate=pl.CostEstimate(
            flops=6 * TOK * D, bytes_accessed=8 * TOK * D, transcendentals=0
        ),
    )(tokens, gain, upstream)


def column_part(low_ref, held_ref, t, half, column):
    mine = lax.axis_index("half")
    part = jnp.zeros((R, TOK), jnp.float32)
    for near in range(QUAD):
        for far in range(2):
            part += lax.dot_general(
                low_ref[near, far, half * R : (half + 1) * R],
                held_ref[t, column, QUAD * (mine ^ far) + near, 1 - half],
                LAST,
                preferred_element_type=jnp.float32,
            )
    return part


def first_project_kernel(keep_ref, got_ref, low_ref, out_ref, held_ref, sem):
    loads = []
    for t, ref in enumerate((keep_ref, got_ref)):
        loads.append(pltpu.make_async_copy(ref, held_ref.at[t], sem.at[t]))
        loads[-1].start()
    for t in range(2):
        loads[t].wait()
        for half in range(2):
            out_ref[t, half * R : (half + 1) * R] = column_part(low_ref, held_ref, t, half, 0)


def second_project_kernel(part_ref, held_ref, low_ref, out_ref):
    for t in range(2):
        for half in range(2):
            rows = slice(half * R, (half + 1) * R)
            out_ref[t, rows] = part_ref[t, rows] + column_part(low_ref, held_ref, t, half, 1)


def first_project(keep, got, low):
    return pl.pallas_call(
        first_project_kernel,
        in_specs=[pl.BlockSpec(memory_space=pl.ANY) for _ in range(2)]
        + [pl.BlockSpec(memory_space=pltpu.VMEM)],
        out_specs=[pl.BlockSpec(memory_space=pltpu.VMEM) for _ in range(2)],
        out_shape=[
            jax.ShapeDtypeStruct((2, 2 * R, TOK), jnp.float32),
            jax.ShapeDtypeStruct((2,) + keep.shape, keep.dtype),
        ],
        scratch_shapes=[pltpu.SemaphoreType.DMA((2,))],
        compiler_params=pltpu.CompilerParams(vmem_limit_bytes=VMEM_LIMIT),
        cost_estimate=pl.CostEstimate(
            flops=4 * TOK * D * R, bytes_accessed=4 * 1024 * 1024, transcendentals=0
        ),
    )(keep, got, low)


EARLY, LATE = (3, 2), (1, 0)


def column_grads(low_ref, feat_ref, out_refs, column):
    me = my_z()
    for nears, out_ref in zip((EARLY, LATE), out_refs, strict=True):
        for i, near in enumerate(nears):
            for far in range(2):
                for half, scale in enumerate((inv_width, inv_rank)):
                    block = feat_ref[:, column, me ^ (near + QUAD * far), 1 - half]
                    block = block.reshape(2 * TOK, OWN)
                    grad = jnp.dot(low_ref[half], block, preferred_element_type=jnp.float32)
                    rows = slice(half * R, (half + 1) * R)
                    out_ref[i, far, rows] = (grad * scale).astype(out_ref.dtype)


def other_kernel(part_ref, got_ref, feat_ref, early_ref, late_ref, low_ref):
    for t in range(2):
        total = part_ref[t] + got_ref[1 - t]
        at = slice(t * TOK, (t + 1) * TOK)
        low_ref[0, :, at] = (total[R:] * inv_rank).astype(jnp.bfloat16)
        low_ref[1, :, at] = (total[:R] * inv_width).astype(jnp.bfloat16)
    column_grads(low_ref, feat_ref, (early_ref, late_ref), 1)


def own_kernel(low_ref, feat_ref, early_ref, late_ref):
    column_grads(low_ref, feat_ref, (early_ref, late_ref), 0)


def early_kernel(own_ref, got_ref, first_ref, second_ref):
    for i, ref in enumerate((first_ref, second_ref)):
        ref[...] = (own_ref[i] + got_ref[i].astype(jnp.float32)).astype(ref.dtype)


def late_kernel(master_ref, own_ref, got_ref, sent_ref, kept_ref):
    sent_ref[...] = (own_ref[0] + got_ref[0].astype(jnp.float32)).astype(sent_ref.dtype)
    kept_ref[0] = own_ref[1, 0] + got_ref[1, 0].astype(jnp.float32) - master_ref[...] / step_size
    kept_ref[1] = own_ref[1, 1] + got_ref[1, 1].astype(jnp.float32)


def small(kernel, outs, *args):
    return pl.pallas_call(
        kernel,
        in_specs=[pl.BlockSpec(memory_space=pltpu.VMEM) for _ in args],
        out_specs=[pl.BlockSpec(memory_space=pltpu.VMEM) for _ in outs],
        out_shape=outs,
        compiler_params=pltpu.CompilerParams(vmem_limit_bytes=VMEM_LIMIT),
        cost_estimate=pl.CostEstimate(
            flops=2 * TOK * D * R, bytes_accessed=1024 * 1024, transcendentals=0
        ),
    )(*args)


def steps(group):
    odd = group % 2
    return 1 + 2 * odd, 3 - 2 * odd


def along_x(array, which):
    pairs = []
    for g in range(GROUPS):
        for x in range(NX):
            pairs.append((g * NX + x, g * NX + (x ^ steps(g)[which])))
    return lax.ppermute(array, ("blk", "x"), pairs)


def swapped(array, by):
    return lax.ppermute(array, ("half", "near"), [(i, i ^ by) for i in range(NZ)])


def my_z():
    return QUAD * lax.axis_index("half") + lax.axis_index("near")


def is_far(group):
    return group % (GROUPS // 2) in (0, GROUPS // 2 - 1)


def first_neighbour(array):
    return lax.ppermute(array, "blk", [(g, g ^ 1) for g in range(GROUPS)])


def second_neighbour(array):
    pairs = []
    for g in range(GROUPS):
        other = (g + 1 if g % 2 else g - 1) % GROUPS
        for z in range(NZ):
            pairs.append((g * NZ + z, other * NZ + (z ^ QUAD if is_far(g) else z)))
    return lax.ppermute(array, ("blk", "half", "near"), pairs)


def local(tokens, norm_gain, adapt_in, adapt_out, upstream):
    wide, narrow = jnp.float32, jnp.bfloat16
    far = ((lax.axis_index("blk") + 1) & (GROUPS // 2 - 1)) < 2

    master = jnp.concatenate([adapt_in[0].T, adapt_out[0].T], axis=0)
    own = master.astype(narrow)
    pair = jnp.stack([own, swapped(own, QUAD)])
    low = lax.all_to_all(jnp.broadcast_to(pair, (QUAD,) + pair.shape), "near", 0, 0, tiled=True)
    other = along_x(low, 1)

    keep, send = prep(tokens[0], norm_gain[None], upstream[0])
    got = along_x(send, 0)
    part, feat = first_project(keep, got, low)
    (part,) = small(
        second_project_kernel, [jax.ShapeDtypeStruct(part.shape, wide)], part, feat, other
    )
    part_got = along_x(part, 0)

    narrow_pieces = jax.ShapeDtypeStruct((2, 2, 2 * R, OWN), narrow)
    wide_pieces = jax.ShapeDtypeStruct(narrow_pieces.shape, wide)
    lowered = jax.ShapeDtypeStruct((2, R, 2 * TOK), narrow)
    *theirs, lowered = small(
        other_kernel, [narrow_pieces, narrow_pieces, lowered], part, part_got, feat
    )
    theirs = [along_x(pieces, 1) for pieces in theirs]
    mine = small(own_kernel, [wide_pieces, wide_pieces], lowered, feat)
    piece = jax.ShapeDtypeStruct((2, 2 * R, OWN), narrow)
    kept = jax.ShapeDtypeStruct(piece.shape, wide)
    sent = small(early_kernel, [piece, piece], mine[0], theirs[0])
    early = [swapped(array, near) for array, near in zip(sent, EARLY, strict=True)]
    sent, quad = small(late_kernel, [piece, kept], master, mine[1], theirs[1])
    for got in early + [swapped(sent, LATE[0])]:
        quad = quad + got.astype(wide)

    sent = quad.astype(narrow)
    second = second_neighbour(sent).astype(wide)
    second = jnp.where(far, second[::-1], second)
    around = quad + first_neighbour(sent).astype(wide) + second
    final = swapped(around[1].astype(narrow), QUAD)
    mixed = []
    for half in range(2):
        rows = slice(half * R, (half + 1) * R)
        total = around[0, rows] + final[rows].astype(wide)
        mixed.append((total * (-step_size / 3.0)).T[None])
    return tuple(mixed)


def solution(mesh):
    axes = ("blk", "half", "near", "x")
    mesh = Mesh(mesh.devices.reshape(GROUPS, 2, QUAD, NX), axes)
    split = P("blk", axes[1:], None)
    in_specs = (split, P(), split, split, split)
    return jax.shard_map(
        local, mesh=mesh, in_specs=in_specs, out_specs=(split, split), check_vma=False
    )
```

```python
import jax
import jax.numpy as jnp
from jax import lax
from jax.experimental import pallas as pl
from jax.experimental.pallas import tpu as pltpu
from jax.sharding import Mesh
from jax.sharding import PartitionSpec as P

D = 8192
R = 64
TOKENS = 4096
GROUPS = 16
NX = 4
NZ = 8
TOK = TOKENS // (NX * NZ)
OWN = D // (NX * NZ)
QUAD = NZ // 2

learning_rate = 4.0
epsilon = 1e-05

inv_width = D ** (-0.5)
inv_rank = R ** (-0.5)
step_size = learning_rate / TOKENS**0.5

ROWS = 32
CHUNKS = TOK // ROWS

LAST = (((1,), (1,)), ((), ()))
VMEM_LIMIT = 32 * 1024 * 1024
DIRECT_LIMIT = 60 * 1024 * 1024


def prep_kernel(tok_ref, gain_ref, up_ref, keep_ref, send_ref, raw_ref, done_ref, in_sem, out_sem):
    sources = (up_ref, tok_ref)
    loads = {}
    for c in range(CHUNKS):
        rows = pl.ds(c * ROWS, ROWS)
        for h in range(2):
            loads[c, h] = pltpu.make_async_copy(
                sources[h].at[rows], raw_ref.at[c, h], in_sem.at[c, h]
            )
            loads[c, h].start()
    me = lax.axis_index("x")
    pair, mate = steps(lax.axis_index("blk"))
    columns = (me, me ^ mate, me ^ pair, me ^ pair ^ mate)
    stores = []
    for c in range(CHUNKS):
        rows = pl.ds(c * ROWS, ROWS)
        for h in range(2):
            loads[c, h].wait()
            if h == 1:
                wide = raw_ref[c, h].astype(jnp.float32)
                scale = lax.rsqrt(jnp.mean(wide * wide, axis=-1, keepdims=True) + epsilon)
            for i, column in enumerate(columns):
                for z in range(NZ):
                    at = pl.ds(pl.multiple_of((z * NX + column) * OWN, OWN), OWN)
                    part = raw_ref[c, h, :, at]
                    if h == 1:
                        part = part.astype(jnp.float32) * scale * gain_ref[:, at]
                    done_ref[c, h, i, z] = part.astype(jnp.bfloat16)
            for i, ref in enumerate((keep_ref, send_ref)):
                src = done_ref.at[c, h, pl.ds(2 * i, 2)]
                stores.append(
                    pltpu.make_async_copy(src, ref.at[:, :, h, rows], out_sem.at[c, h, i])
                )
                stores[-1].start()
    for copy in stores:
        copy.wait()


def prep(tokens, gain, upstream):
    out = jax.ShapeDtypeStruct((2, NZ, 2, TOK, OWN), jnp.bfloat16)
    return pl.pallas_call(
        prep_kernel,
        in_specs=[
            pl.BlockSpec(memory_space=pl.ANY),
            pl.BlockSpec(memory_space=pltpu.VMEM),
            pl.BlockSpec(memory_space=pl.ANY),
        ],
        out_specs=[pl.BlockSpec(memory_space=pl.ANY) for _ in range(2)],
        out_shape=[out, out],
        scratch_shapes=[
            pltpu.VMEM((CHUNKS, 2, ROWS, D), jnp.bfloat16),
            pltpu.VMEM((CHUNKS, 2, 4, NZ, ROWS, OWN), jnp.bfloat16),
            pltpu.SemaphoreType.DMA((CHUNKS, 2)),
            pltpu.SemaphoreType.DMA((CHUNKS, 2, 2)),
        ],
        compiler_params=pltpu.CompilerParams(vmem_limit_bytes=DIRECT_LIMIT),
        cost_estimate=pl.CostEstimate(
            flops=6 * TOK * D, bytes_accessed=8 * TOK * D, transcendentals=0
        ),
    )(tokens, gain, upstream)


def column_part(low_ref, held_ref, t, half, column):
    mine = lax.axis_index("half")
    part = jnp.zeros((R, TOK), jnp.float32)
    for near in range(QUAD):
        for far in range(2):
            part += lax.dot_general(
                low_ref[near, far, half * R : (half + 1) * R],
                held_ref[t, column, QUAD * (mine ^ far) + near, 1 - half],
                LAST,
                preferred_element_type=jnp.float32,
            )
    return part


def first_project_kernel(keep_ref, got_ref, low_ref, out_ref, held_ref, sem):
    loads = []
    for t, ref in enumerate((keep_ref, got_ref)):
        loads.append(pltpu.make_async_copy(ref, held_ref.at[t], sem.at[t]))
        loads[-1].start()
    for t in range(2):
        loads[t].wait()
        for half in range(2):
            out_ref[t, half * R : (half + 1) * R] = column_part(low_ref, held_ref, t, half, 0)


def second_project_kernel(part_ref, held_ref, low_ref, out_ref):
    for t in range(2):
        for half in range(2):
            rows = slice(half * R, (half + 1) * R)
            out_ref[t, rows] = part_ref[t, rows] + column_part(low_ref, held_ref, t, half, 1)


def first_project(keep, got, low):
    return pl.pallas_call(
        first_project_kernel,
        in_specs=[pl.BlockSpec(memory_space=pl.ANY) for _ in range(2)]
        + [pl.BlockSpec(memory_space=pltpu.VMEM)],
        out_specs=[pl.BlockSpec(memory_space=pltpu.VMEM) for _ in range(2)],
        out_shape=[
            jax.ShapeDtypeStruct((2, 2 * R, TOK), jnp.float32),
            jax.ShapeDtypeStruct((2,) + keep.shape, keep.dtype),
        ],
        scratch_shapes=[pltpu.SemaphoreType.DMA((2,))],
        compiler_params=pltpu.CompilerParams(vmem_limit_bytes=VMEM_LIMIT),
        cost_estimate=pl.CostEstimate(
            flops=4 * TOK * D * R, bytes_accessed=4 * 1024 * 1024, transcendentals=0
        ),
    )(keep, got, low)


EARLY, LATE = (3, 2), (1, 0)


def column_grads(low_ref, feat_ref, out_ref, column, nears):
    me = my_z()
    for i, near in enumerate(nears):
        for far in range(2):
            for half, scale in enumerate((inv_width, inv_rank)):
                block = feat_ref[:, column, me ^ (near + QUAD * far), 1 - half]
                block = block.reshape(2 * TOK, OWN)
                grad = jnp.dot(low_ref[half], block, preferred_element_type=jnp.float32)
                rows = slice(half * R, (half + 1) * R)
                out_ref[i, far, rows] = (grad * scale).astype(out_ref.dtype)


def other_early_kernel(part_ref, got_ref, feat_ref, out_ref, low_ref):
    for t in range(2):
        total = part_ref[t] + got_ref[1 - t]
        at = slice(t * TOK, (t + 1) * TOK)
        low_ref[0, :, at] = (total[R:] * inv_rank).astype(jnp.bfloat16)
        low_ref[1, :, at] = (total[:R] * inv_width).astype(jnp.bfloat16)
    column_grads(low_ref, feat_ref, out_ref, 1, EARLY)


def other_late_kernel(low_ref, feat_ref, out_ref):
    column_grads(low_ref, feat_ref, out_ref, 1, LATE)


def own_kernel(low_ref, feat_ref, early_ref, late_ref):
    column_grads(low_ref, feat_ref, early_ref, 0, EARLY)
    column_grads(low_ref, feat_ref, late_ref, 0, LATE)


def early_kernel(own_ref, got_ref, first_ref, second_ref):
    for i, ref in enumerate((first_ref, second_ref)):
        ref[...] = (own_ref[i] + got_ref[i].astype(jnp.float32)).astype(ref.dtype)


def late_kernel(master_ref, own_ref, got_ref, sent_ref, kept_ref):
    sent_ref[...] = (own_ref[0] + got_ref[0].astype(jnp.float32)).astype(sent_ref.dtype)
    kept_ref[0] = own_ref[1, 0] + got_ref[1, 0].astype(jnp.float32) - master_ref[...] / step_size
    kept_ref[1] = own_ref[1, 1] + got_ref[1, 1].astype(jnp.float32)


def small(kernel, outs, *args):
    return pl.pallas_call(
        kernel,
        in_specs=[pl.BlockSpec(memory_space=pltpu.VMEM) for _ in args],
        out_specs=[pl.BlockSpec(memory_space=pltpu.VMEM) for _ in outs],
        out_shape=outs,
        compiler_params=pltpu.CompilerParams(vmem_limit_bytes=VMEM_LIMIT),
        cost_estimate=pl.CostEstimate(
            flops=2 * TOK * D * R, bytes_accessed=1024 * 1024, transcendentals=0
        ),
    )(*args)


def steps(group):
    odd = group % 2
    return 1 + 2 * odd, 3 - 2 * odd


def along_x(array, which):
    pairs = []
    for g in range(GROUPS):
        for x in range(NX):
            pairs.append((g * NX + x, g * NX + (x ^ steps(g)[which])))
    return lax.ppermute(array, ("blk", "x"), pairs)


def swapped(array, by):
    return lax.ppermute(array, ("half", "near"), [(i, i ^ by) for i in range(NZ)])


def my_z():
    return QUAD * lax.axis_index("half") + lax.axis_index("near")


def is_far(group):
    return group % (GROUPS // 2) in (0, GROUPS // 2 - 1)


def first_neighbour(array):
    return lax.ppermute(array, "blk", [(g, g ^ 1) for g in range(GROUPS)])


def second_neighbour(array):
    pairs = []
    for g in range(GROUPS):
        other = (g + 1 if g % 2 else g - 1) % GROUPS
        for z in range(NZ):
            pairs.append((g * NZ + z, other * NZ + (z ^ QUAD if is_far(g) else z)))
    return lax.ppermute(array, ("blk", "half", "near"), pairs)


def local(tokens, norm_gain, adapt_in, adapt_out, upstream):
    wide, narrow = jnp.float32, jnp.bfloat16
    far = ((lax.axis_index("blk") + 1) & (GROUPS // 2 - 1)) < 2

    master = jnp.concatenate([adapt_in[0].T, adapt_out[0].T], axis=0)
    own = master.astype(narrow)
    pair = jnp.stack([own, swapped(own, QUAD)])
    low = lax.all_to_all(jnp.broadcast_to(pair, (QUAD,) + pair.shape), "near", 0, 0, tiled=True)
    other = along_x(low, 1)

    keep, send = prep(tokens[0], norm_gain[None], upstream[0])
    got = along_x(send, 0)
    part, feat = first_project(keep, got, low)
    (part,) = small(
        second_project_kernel, [jax.ShapeDtypeStruct(part.shape, wide)], part, feat, other
    )
    part_got = along_x(part, 0)

    narrow_pieces = jax.ShapeDtypeStruct((2, 2, 2 * R, OWN), narrow)
    wide_pieces = jax.ShapeDtypeStruct(narrow_pieces.shape, wide)
    lowered = jax.ShapeDtypeStruct((2, R, 2 * TOK), narrow)
    early, lowered = small(other_early_kernel, [narrow_pieces, lowered], part, part_got, feat)
    (late,) = small(other_late_kernel, [narrow_pieces], lowered, feat)
    theirs = [along_x(early, 1), along_x(late, 1)]
    mine = small(own_kernel, [wide_pieces, wide_pieces], lowered, feat)
    piece = jax.ShapeDtypeStruct((2, 2 * R, OWN), narrow)
    kept = jax.ShapeDtypeStruct(piece.shape, wide)
    sent = small(early_kernel, [piece, piece], mine[0], theirs[0])
    early = [swapped(array, near) for array, near in zip(sent, EARLY, strict=True)]
    sent, quad = small(late_kernel, [piece, kept], master, mine[1], theirs[1])
    for got in early + [swapped(sent, LATE[0])]:
        quad = quad + got.astype(wide)

    sent = quad.astype(narrow)
    second = second_neighbour(sent).astype(wide)
    second = jnp.where(far, second[::-1], second)
    around = quad + first_neighbour(sent).astype(wide) + second
    final = swapped(around[1].astype(narrow), QUAD)
    mixed = []
    for half in range(2):
        rows = slice(half * R, (half + 1) * R)
        total = around[0, rows] + final[rows].astype(wide)
        mixed.append((total * (-step_size / 3.0)).T[None])
    return tuple(mixed)


def solution(mesh):
    axes = ("blk", "half", "near", "x")
    mesh = Mesh(mesh.devices.reshape(GROUPS, 2, QUAD, NX), axes)
    split = P("blk", axes[1:], None)
    in_specs = (split, P(), split, split, split)
    return jax.shard_map(
        local, mesh=mesh, in_specs=in_specs, out_specs=(split, split), check_vma=False
    )
```

```python
import jax
import jax.numpy as jnp
from jax import lax
from jax.experimental import pallas as pl
from jax.experimental.pallas import tpu as pltpu
from jax.sharding import Mesh
from jax.sharding import PartitionSpec as P

D = 8192
R = 64
TOKENS = 4096
GROUPS = 16
NX = 4
NZ = 8
TOK = TOKENS // (NX * NZ)
OWN = D // (NX * NZ)
QUAD = NZ // 2

learning_rate = 4.0
epsilon = 1e-05

inv_width = D ** (-0.5)
inv_rank = R ** (-0.5)
step_size = learning_rate / TOKENS**0.5

ROWS = 64
CHUNKS = TOK // ROWS

LAST = (((1,), (1,)), ((), ()))
VMEM_LIMIT = 32 * 1024 * 1024
DIRECT_LIMIT = 60 * 1024 * 1024


def prep_kernel(tok_ref, gain_ref, up_ref, keep_ref, send_ref, raw_ref, done_ref, in_sem, out_sem):
    sources = (up_ref, tok_ref)
    loads = {}
    for c in range(CHUNKS):
        rows = pl.ds(c * ROWS, ROWS)
        for h in range(2):
            loads[c, h] = pltpu.make_async_copy(
                sources[h].at[rows], raw_ref.at[c, h], in_sem.at[c, h]
            )
            loads[c, h].start()
    me = lax.axis_index("x")
    pair, mate = steps(lax.axis_index("blk"))
    columns = (me, me ^ mate, me ^ pair, me ^ pair ^ mate)
    stores = []
    for c in range(CHUNKS):
        rows = pl.ds(c * ROWS, ROWS)
        for h in range(2):
            loads[c, h].wait()
            if h == 1:
                wide = raw_ref[c, h].astype(jnp.float32)
                scale = lax.rsqrt(jnp.mean(wide * wide, axis=-1, keepdims=True) + epsilon)
            for i, column in enumerate(columns):
                for z in range(NZ):
                    at = pl.ds(pl.multiple_of((z * NX + column) * OWN, OWN), OWN)
                    part = raw_ref[c, h, :, at]
                    if h == 1:
                        part = part.astype(jnp.float32) * scale * gain_ref[:, at]
                    done_ref[c, h, i, z] = part.astype(jnp.bfloat16)
            for i, ref in enumerate((keep_ref, send_ref)):
                src = done_ref.at[c, h, pl.ds(2 * i, 2)]
                stores.append(
                    pltpu.make_async_copy(src, ref.at[:, :, h, rows], out_sem.at[c, h, i])
                )
                stores[-1].start()
    for copy in stores:
        copy.wait()


def prep(tokens, gain, upstream):
    out = jax.ShapeDtypeStruct((2, NZ, 2, TOK, OWN), jnp.bfloat16)
    return pl.pallas_call(
        prep_kernel,
        in_specs=[
            pl.BlockSpec(memory_space=pl.ANY),
            pl.BlockSpec(memory_space=pltpu.VMEM),
            pl.BlockSpec(memory_space=pl.ANY),
        ],
        out_specs=[pl.BlockSpec(memory_space=pl.ANY) for _ in range(2)],
        out_shape=[out, out],
        scratch_shapes=[
            pltpu.VMEM((CHUNKS, 2, ROWS, D), jnp.bfloat16),
            pltpu.VMEM((CHUNKS, 2, 4, NZ, ROWS, OWN), jnp.bfloat16),
            pltpu.SemaphoreType.DMA((CHUNKS, 2)),
            pltpu.SemaphoreType.DMA((CHUNKS, 2, 2)),
        ],
        compiler_params=pltpu.CompilerParams(vmem_limit_bytes=DIRECT_LIMIT),
        cost_estimate=pl.CostEstimate(
            flops=6 * TOK * D, bytes_accessed=8 * TOK * D, transcendentals=0
        ),
    )(tokens, gain, upstream)


def column_part(low_ref, held_ref, t, half, column):
    mine = lax.axis_index("half")
    part = jnp.zeros((R, TOK), jnp.float32)
    for near in range(QUAD):
        for far in range(2):
            part += lax.dot_general(
                low_ref[near, far, half * R : (half + 1) * R],
                held_ref[t, column, QUAD * (mine ^ far) + near, 1 - half],
                LAST,
                preferred_element_type=jnp.float32,
            )
    return part


def first_project_kernel(keep_ref, got_ref, low_ref, out_ref, held_ref, sem):
    loads = []
    for t, ref in enumerate((keep_ref, got_ref)):
        loads.append(pltpu.make_async_copy(ref, held_ref.at[t], sem.at[t]))
        loads[-1].start()
    for t in range(2):
        loads[t].wait()
        for half in range(2):
            out_ref[t, half * R : (half + 1) * R] = column_part(low_ref, held_ref, t, half, 0)


def second_project_kernel(part_ref, held_ref, low_ref, out_ref):
    for t in range(2):
        for half in range(2):
            rows = slice(half * R, (half + 1) * R)
            out_ref[t, rows] = part_ref[t, rows] + column_part(low_ref, held_ref, t, half, 1)


def first_project(keep, got, low):
    return pl.pallas_call(
        first_project_kernel,
        in_specs=[pl.BlockSpec(memory_space=pl.ANY) for _ in range(2)]
        + [pl.BlockSpec(memory_space=pltpu.VMEM)],
        out_specs=[pl.BlockSpec(memory_space=pltpu.VMEM) for _ in range(2)],
        out_shape=[
            jax.ShapeDtypeStruct((2, 2 * R, TOK), jnp.float32),
            jax.ShapeDtypeStruct((2,) + keep.shape, keep.dtype),
        ],
        scratch_shapes=[pltpu.SemaphoreType.DMA((2,))],
        compiler_params=pltpu.CompilerParams(vmem_limit_bytes=VMEM_LIMIT),
        cost_estimate=pl.CostEstimate(
            flops=4 * TOK * D * R, bytes_accessed=4 * 1024 * 1024, transcendentals=0
        ),
    )(keep, got, low)


EARLY, LATE = (3, 2), (1, 0)


def column_grads(low_ref, feat_ref, out_ref, column, nears):
    me = my_z()
    for i, near in enumerate(nears):
        for far in range(2):
            for half, scale in enumerate((inv_width, inv_rank)):
                block = feat_ref[:, column, me ^ (near + QUAD * far), 1 - half]
                block = block.reshape(2 * TOK, OWN)
                grad = jnp.dot(low_ref[half], block, preferred_element_type=jnp.float32)
                rows = slice(half * R, (half + 1) * R)
                out_ref[i, far, rows] = (grad * scale).astype(out_ref.dtype)


def other_early_kernel(part_ref, got_ref, feat_ref, out_ref, low_ref):
    for t in range(2):
        total = part_ref[t] + got_ref[1 - t]
        at = slice(t * TOK, (t + 1) * TOK)
        low_ref[0, :, at] = (total[R:] * inv_rank).astype(jnp.bfloat16)
        low_ref[1, :, at] = (total[:R] * inv_width).astype(jnp.bfloat16)
    column_grads(low_ref, feat_ref, out_ref, 1, EARLY)


def other_late_kernel(low_ref, feat_ref, out_ref):
    column_grads(low_ref, feat_ref, out_ref, 1, LATE)


def own_kernel(low_ref, feat_ref, early_ref, late_ref):
    column_grads(low_ref, feat_ref, early_ref, 0, EARLY)
    column_grads(low_ref, feat_ref, late_ref, 0, LATE)


def early_kernel(own_ref, got_ref, first_ref, second_ref):
    for i, ref in enumerate((first_ref, second_ref)):
        ref[...] = (own_ref[i] + got_ref[i].astype(jnp.float32)).astype(ref.dtype)


def late_kernel(master_ref, own_ref, got_ref, sent_ref, kept_ref):
    sent_ref[...] = (own_ref[0] + got_ref[0].astype(jnp.float32)).astype(sent_ref.dtype)
    kept_ref[0] = own_ref[1, 0] + got_ref[1, 0].astype(jnp.float32) - master_ref[...] / step_size
    kept_ref[1] = own_ref[1, 1] + got_ref[1, 1].astype(jnp.float32)


def small(kernel, outs, *args):
    return pl.pallas_call(
        kernel,
        in_specs=[pl.BlockSpec(memory_space=pltpu.VMEM) for _ in args],
        out_specs=[pl.BlockSpec(memory_space=pltpu.VMEM) for _ in outs],
        out_shape=outs,
        compiler_params=pltpu.CompilerParams(vmem_limit_bytes=VMEM_LIMIT),
        cost_estimate=pl.CostEstimate(
            flops=2 * TOK * D * R, bytes_accessed=1024 * 1024, transcendentals=0
        ),
    )(*args)


def steps(group):
    odd = group % 2
    return 1 + 2 * odd, 3 - 2 * odd


def along_x(array, which):
    pairs = []
    for g in range(GROUPS):
        for x in range(NX):
            pairs.append((g * NX + x, g * NX + (x ^ steps(g)[which])))
    return lax.ppermute(array, ("blk", "x"), pairs)


def swapped(array, by):
    return lax.ppermute(array, ("half", "near"), [(i, i ^ by) for i in range(NZ)])


def my_z():
    return QUAD * lax.axis_index("half") + lax.axis_index("near")


def is_far(group):
    return group % (GROUPS // 2) in (0, GROUPS // 2 - 1)


def first_neighbour(array):
    return lax.ppermute(array, "blk", [(g, g ^ 1) for g in range(GROUPS)])


def second_neighbour(array):
    pairs = []
    for g in range(GROUPS):
        other = (g + 1 if g % 2 else g - 1) % GROUPS
        for z in range(NZ):
            pairs.append((g * NZ + z, other * NZ + (z ^ QUAD if is_far(g) else z)))
    return lax.ppermute(array, ("blk", "half", "near"), pairs)


def local(tokens, norm_gain, adapt_in, adapt_out, upstream):
    wide, narrow = jnp.float32, jnp.bfloat16
    far = ((lax.axis_index("blk") + 1) & (GROUPS // 2 - 1)) < 2

    master = jnp.concatenate([adapt_in[0].T, adapt_out[0].T], axis=0)
    own = master.astype(narrow)
    pair = jnp.stack([own, swapped(own, QUAD)])
    low = lax.all_to_all(jnp.broadcast_to(pair, (QUAD,) + pair.shape), "near", 0, 0, tiled=True)
    other = along_x(low, 1)

    keep, send = prep(tokens[0], norm_gain[None], upstream[0])
    got = along_x(send, 0)
    part, feat = first_project(keep, got, low)
    (part,) = small(
        second_project_kernel, [jax.ShapeDtypeStruct(part.shape, wide)], part, feat, other
    )
    part_got = along_x(part, 0)

    narrow_pieces = jax.ShapeDtypeStruct((2, 2, 2 * R, OWN), narrow)
    wide_pieces = jax.ShapeDtypeStruct(narrow_pieces.shape, wide)
    lowered = jax.ShapeDtypeStruct((2, R, 2 * TOK), narrow)
    early, lowered = small(other_early_kernel, [narrow_pieces, lowered], part, part_got, feat)
    (late,) = small(other_late_kernel, [narrow_pieces], lowered, feat)
    theirs = [along_x(early, 1), along_x(late, 1)]
    mine = small(own_kernel, [wide_pieces, wide_pieces], lowered, feat)
    piece = jax.ShapeDtypeStruct((2, 2 * R, OWN), narrow)
    kept = jax.ShapeDtypeStruct(piece.shape, wide)
    sent = small(early_kernel, [piece, piece], mine[0], theirs[0])
    early = [swapped(array, near) for array, near in zip(sent, EARLY, strict=True)]
    sent, quad = small(late_kernel, [piece, kept], master, mine[1], theirs[1])
    for got in early + [swapped(sent, LATE[0])]:
        quad = quad + got.astype(wide)

    sent = quad.astype(narrow)
    second = second_neighbour(sent).astype(wide)
    second = jnp.where(far, second[::-1], second)
    around = quad + first_neighbour(sent).astype(wide) + second
    final = swapped(around[1].astype(narrow), QUAD)
    mixed = []
    for half in range(2):
        rows = slice(half * R, (half + 1) * R)
        total = around[0, rows] + final[rows].astype(wide)
        mixed.append((total * (-step_size / 3.0)).T[None])
    return tuple(mixed)


def solution(mesh):
    axes = ("blk", "half", "near", "x")
    mesh = Mesh(mesh.devices.reshape(GROUPS, 2, QUAD, NX), axes)
    split = P("blk", axes[1:], None)
    in_specs = (split, P(), split, split, split)
    return jax.shard_map(
        local, mesh=mesh, in_specs=in_specs, out_specs=(split, split), check_vma=False
    )
```
